128 devices in a mesh: site: 8 (over y, core), op: 16 (over x, z).
Axes of the slice: x: 4, y: 4, z: 4, core: 2. Of those that a mesh axis runs over, the one named last changes fastest.
Arguments:
- psi: bfloat16 [8, 16, 256, 256], P('site'), may hold values from -16 to 16
- diagonal: float32 [8, 16, 256, 256], P('site'), may hold values from 1 to 32
- left_step: float32 [8, 256, 256], P('site'), may hold values from -0.375 to 0.375
- right_step: float32 [8, 256, 256], P('site'), may hold values from -0.375 to 0.375
- left_env: bfloat16 [64, 256, 256], P('op'), may hold values from -1.125 to 1.125
- right_env: bfloat16 [64, 256, 256], P('op'), may hold values from -1.125 to 1.125
- src_block: int32 [64], P('op'), may hold values from 0 to 15
- dst_block: int32 [64], P('op'), may hold values from 0 to 15
Outputs:
- ground: float32 [8, 16, 256, 256], P('site', 'op')
The draws below stay inside these ranges and needn't reach their ends.
All inputs are finite; a program needn't handle non-finite values.
Results may differ from the reference program's by a relative error of at most 0.0078.
Values may be sent and summed in bfloat16 or wider, within the bound.
No kernel may reach another device: no remote copies, remote signals or barrier semaphores. Data moves between devices by JAX's collectives and lax.ppermute only.
A program may use at most 128 MiB of HBM per device.

```python
import math
import jax
import jax.numpy as jnp
from jax import lax

BLK = 256
ITERS = 2
NB = 16
TERMS = 64
SITES = 8
N_SITE = 8


def env_values(key, count):
    spread = 3.0 / math.sqrt(BLK)
    base = jax.random.normal(key, (count, BLK, BLK), jnp.float32)
    return jnp.clip(base * spread, -6.0 * spread, 6.0 * spread)


def draw_psi(key, part):
    key = jax.random.fold_in(key, 11)
    key_level, key_base = jax.random.split(key)
    levels = jnp.exp(jax.random.uniform(key_level, (SITES, NB, 1, BLK), jnp.float32, -2.5, 2.5))
    base = jax.random.normal(key_base, (SITES, NB, BLK, BLK), jnp.float32)
    return jnp.clip(base * levels, -16.0, 16.0).astype(jnp.bfloat16)


def draw_diagonal(key, part):
    key = jax.random.fold_in(key, 23)
    key_level, key_cell = jax.random.split(key)
    levels = jnp.exp(jax.random.uniform(key_level, (SITES, NB, 1, BLK), jnp.float32, 0.0, math.log(16.0)))
    factor = jnp.exp(jax.random.uniform(key_cell, (SITES, NB, BLK, BLK), jnp.float32, 0.0, math.log(2.0)))
    return jnp.clip(levels * factor, 1.0, 32.0)


def draw_left_env(key, part):
    key = jax.random.fold_in(key, 37)
    return env_values(key, TERMS).astype(jnp.bfloat16)


def draw_right_env(key, part):
    key = jax.random.fold_in(key, 41)
    return env_values(key, TERMS).astype(jnp.bfloat16)


def place_ends(entries, rng, low, top_value):
    spot = [jax.random.randint(jax.random.fold_in(rng, axis), (), 0, length) for axis, length in enumerate(entries.shape)]
    longest = entries.shape.index(max(entries.shape))
    beside = spot[:longest] + [(spot[longest] + 1) % entries.shape[longest]] + spot[longest + 1:]
    return entries.at[tuple(spot)].set(low).at[tuple(beside)].set(top_value)


def shard_levels(rng, shape, cuts, low, high):
    loudness = 1.0
    for dim, blocks in cuts:
        steps = jax.random.uniform(jax.random.fold_in(jax.random.fold_in(rng, 6), dim), (blocks,), jnp.float32, low / len(cuts), high / len(cuts))
        loudness = loudness * jnp.repeat(jnp.exp(steps), shape[dim] // blocks).reshape((-1,) + (1,) * (len(shape) - 1 - dim))
    return loudness


def noise(own_key, extent, width, bound, shards=(), held_as=jnp.bfloat16):
    result = width * jax.random.normal(own_key, extent, jnp.float32)
    if shards:
        result = result * shard_levels(own_key, extent, shards, -0.22, 0.18)
    return jnp.clip(result, -bound, bound).astype(held_as)


def setup_inputs(seed: int = 0) -> dict:
    splits = jax.random.split(jax.random.key(seed), 9)
    return {
        "psi": draw_psi(jax.random.fold_in(splits[8], 71), 0),
        "diagonal": draw_diagonal(jax.random.fold_in(splits[8], 71), 0),
        "left_step": noise(splits[2], (SITES, BLK, BLK), BLK ** -0.5, 0.375, ((0, 8),), jnp.float32),
        "right_step": noise(splits[3], (SITES, BLK, BLK), BLK ** -0.5, 0.375, ((0, 8),), jnp.float32),
        "left_env": draw_left_env(jax.random.fold_in(splits[8], 71), 0),
        "right_env": draw_right_env(jax.random.fold_in(splits[8], 71), 0),
        "src_block": place_ends(jax.random.randint(splits[6], (TERMS,), 0, NB), jax.random.fold_in(splits[6], 1), 0, NB - 1).astype(jnp.int32),
        "dst_block": place_ends(jax.random.randint(splits[7], (TERMS,), 0, NB), jax.random.fold_in(splits[7], 1), 0, NB - 1).astype(jnp.int32),
    }


HIGH = lax.Precision.HIGHEST

def build_envs(left_env, right_env, lq, rq):
    lf = lq.astype(jnp.float32)
    rf = rq.astype(jnp.float32)
    ltmp = jnp.einsum('tij,jk->tik', left_env.astype(jnp.float32), lf).astype(jnp.bfloat16)
    lenv = jnp.einsum('ji,tjk->tik', lf, ltmp.astype(jnp.float32)).astype(jnp.bfloat16)
    rtmp = jnp.einsum('tij,kj->tik', right_env.astype(jnp.float32), rf).astype(jnp.bfloat16)
    renv = jnp.einsum('ij,tjk->tik', rf, rtmp.astype(jnp.float32)).astype(jnp.bfloat16)
    return (lenv, renv)

def apply_ham(vec, diag, lenv, renv, src_block, dst_block):
    vb = vec.astype(jnp.bfloat16).astype(jnp.float32)
    lf = lenv.astype(jnp.float32)
    rf = renv.astype(jnp.float32)
    forward = jnp.einsum('tij,tjk->tik', vb[src_block], rf).astype(jnp.bfloat16).astype(jnp.float32)
    backward = jnp.einsum('tij,tkj->tik', vb[dst_block], rf).astype(jnp.bfloat16).astype(jnp.float32)
    first = jnp.einsum('tij,tjk->tik', lf, forward)
    second = jnp.einsum('tji,tjk->tik', lf, backward)
    blocks = jnp.arange(vec.shape[0], dtype=jnp.int32)
    dst_hit = (dst_block[None, :] == blocks[:, None]).astype(jnp.float32)
    src_hit = (src_block[None, :] == blocks[:, None]).astype(jnp.float32)
    total = jnp.einsum('nt,tij->nij', dst_hit, first, precision=HIGH)
    total = total + jnp.einsum('nt,tij->nij', src_hit, second, precision=HIGH)
    return diag * vec + total

def solve_site(start, diag, lenv, renv, src_block, dst_block):
    x = start.astype(jnp.float32)
    x = x / jnp.sqrt(jnp.sum(x * x) + 1e-12)
    h = apply_ham(x, diag, lenv, renv, src_block, dst_block)
    for step in range(ITERS):
        theta = jnp.sum(x * h)
        t = (h - theta * x) / diag
        t = t - jnp.sum(x * t) * x
        t = t / jnp.sqrt(jnp.sum(t * t) + 1e-12)
        g = apply_ham(t, diag, lenv, renv, src_block, dst_block)
        cross = jnp.sum(x * g)
        curve = jnp.sum(t * g)
        lowered = (curve - theta) / 2 + jnp.sqrt(((theta - curve) / 2) ** 2 + cross * cross)
        norm_pair = jnp.sqrt(lowered * lowered + cross * cross)
        keep = lowered / norm_pair
        move = cross / norm_pair
        x = keep * x - move * t
        h = keep * h - move * g
    return x * jnp.sqrt(jnp.float32(NB * BLK * BLK))

def reference(psi, diagonal, left_step, right_step, left_env, right_env, src_block, dst_block):
    eye = jnp.eye(BLK, dtype=jnp.float32)
    lsteps = eye[None] + 0.3 * left_step
    rsteps = eye[None] + 0.3 * right_step
    lefts = []
    running = eye
    for s in range(N_SITE):
        lefts.append(running)
        running = jnp.dot(running, lsteps[s], precision=HIGH)
    rights = [eye] * N_SITE
    running = eye
    for s in reversed(range(N_SITE)):
        rights[s] = running
        running = jnp.dot(rsteps[s], running, precision=HIGH)
    results = []
    for s in range(N_SITE):
        lenv, renv = build_envs(left_env, right_env, lefts[s].astype(jnp.bfloat16), rights[s].astype(jnp.bfloat16))
        results.append(solve_site(psi[s], diagonal[s], lenv, renv, src_block, dst_block))
    return jnp.stack(results)
```

```python
import jax
import jax.numpy as jnp
from jax import lax
from jax.experimental import pallas as pl
from jax.experimental.pallas import tpu as pltpu
from jax.sharding import PartitionSpec as P

ITERS = 2
BLK = 256
NB = 16
BF16 = jnp.bfloat16
F32 = jnp.float32
HIGH = lax.Precision.HIGHEST
MIB = 1 << 20

XA, XB, ZA, ZB = (1, 0), (3, 0), (0, 1), (0, 3)
ORDERS = ((XA, ZA, XB, ZB), (ZA, XB, ZB, XA), (XB, ZB, XA, ZA), (ZB, XA, ZA, XB))


def swap_op(value, mask):
    mx, mz = mask
    pairs = [
        (x * 4 + z, (x ^ mx) * 4 + (z ^ mz)) for x in range(4) for z in range(4)
    ]
    return lax.ppermute(value, "op", pairs)


def swap_core(value):
    return lax.ppermute(value, "site", [(i, i ^ 1) for i in range(8)])


def dot(a, b):
    return jnp.dot(a, b, preferred_element_type=F32)


def dot_nt(a, b):
    return lax.dot_general(a, b, (((1,), (1,)), ((), ())), preferred_element_type=F32)


def dot_tn(a, b):
    return lax.dot_general(a, b, (((0,), (0,)), ((), ())), preferred_element_type=F32)


def dot_high(a, b):
    return jnp.dot(a, b, precision=HIGH, preferred_element_type=F32)


def identity():
    rows = lax.broadcasted_iota(jnp.int32, (BLK, BLK), 0)
    cols = lax.broadcasted_iota(jnp.int32, (BLK, BLK), 1)
    return jnp.where(rows == cols, 1.0, 0.0).astype(F32)


def pair_kernel(site_ref, own_ref, other_ref, out_ref):
    eye = identity()
    core = site_ref[0] % 2

    @pl.when(core == 0)
    def _():
        out_ref[...] = dot_high(eye + 0.3 * own_ref[0], eye + 0.3 * other_ref[0])

    @pl.when(core == 1)
    def _():
        out_ref[...] = dot_high(eye + 0.3 * other_ref[1], eye + 0.3 * own_ref[1])


def pair_product(site, own, other):
    vmem = pl.BlockSpec(memory_space=pltpu.VMEM)
    return pl.pallas_call(
        pair_kernel,
        out_shape=jax.ShapeDtypeStruct((BLK, BLK), F32),
        in_specs=[pl.BlockSpec(memory_space=pltpu.SMEM), vmem, vmem],
        out_specs=vmem,
        cost_estimate=pl.CostEstimate(flops=12 * BLK**3, bytes_accessed=MIB, transcendentals=0),
    )(site, own, other)


def chain_kernel(site_ref, other_ref, m1, m2, m3, n1, n2, n3, lq_ref, rq_ref):
    eye = identity()
    site = site_ref[0]
    core, y = site % 2, site // 2

    def chain(left, right):
        lefts = [jnp.where(y >= k + 1, left[k][...], eye) for k in range(3)]
        rights = [jnp.where(y + k + 1 <= 3, right[k][...], eye) for k in range(3)]
        s_part = jnp.where(core == 1, eye + 0.3 * other_ref[0], eye)
        t_part = jnp.where(core == 0, eye + 0.3 * other_ref[1], eye)
        a = dot_high(lefts[2], lefts[1])
        b = dot_high(lefts[0], s_part)
        c = dot_high(t_part, rights[0])
        d = dot_high(rights[1], rights[2])
        lq_ref[...] = dot_high(a, b).astype(BF16)
        rq_ref[...] = dot_high(c, d).astype(BF16)

    @pl.when(core == 0)
    def _():
        chain((m1, m2, m3), (n1, n2, n3))

    @pl.when(core == 1)
    def _():
        chain((n1, n2, n3), (m1, m2, m3))


def chain_products(site, other, received, across):
    vmem = pl.BlockSpec(memory_space=pltpu.VMEM)
    out = jax.ShapeDtypeStruct((BLK, BLK), BF16)
    return pl.pallas_call(
        chain_kernel,
        out_shape=(out, out),
        in_specs=[pl.BlockSpec(memory_space=pltpu.SMEM)] + [vmem] * 7,
        out_specs=(vmem, vmem),
        cost_estimate=pl.CostEstimate(flops=72 * BLK**3, bytes_accessed=2 * MIB, transcendentals=0),
    )(site, other, *received, *across)


def transfers(site, left_step, right_step):
    own = jnp.concatenate([left_step, right_step], 0)
    other = swap_core(own)
    mine = pair_product(site, own, other)
    received = []
    for k in (1, 2, 3):
        pairs = [(2 * y, 2 * (y + k)) for y in range(4 - k)]
        pairs += [(2 * y + 1, 2 * (y - k) + 1) for y in range(k, 4)]
        received.append(lax.ppermute(mine, "site", pairs))
    across = [swap_core(r) for r in received]
    return chain_products(site, other, received, across)


def gather_terms(parts):
    held = [p[None] for p in parts]
    for stage in range(3):
        got = [swap_op(h, order[stage]) for h, order in zip(held, ORDERS)]
        held = [jnp.concatenate(pair, 0) for pair in zip(held, got)]
    last = [swap_op(h, order[3]) for h, order in zip(held, ORDERS)]
    return held, last, [swap_core(h) for h in held], [swap_core(h) for h in last]


def term_slots(k, place):
    pick, t, j = k // 32, (k // 16) % 2, k % 16
    b0, b1, b2, b3 = j % 2, (j // 2) % 2, (j // 4) % 2, j // 8
    xa, xb = jnp.where(t == 0, b0, b2), jnp.where(t == 0, b2, b0)
    za, zb = jnp.where(t == 0, b1, b3), jnp.where(t == 0, b3, b1)
    x = jnp.bitwise_xor(place[0], xa + xb * 3 - 2 * xa * xb)
    z = jnp.bitwise_xor(place[1], za + zb * 3 - 2 * za * zb)
    core = jnp.bitwise_xor(place[2], pick)
    right = k - j + j // 2 + 8 * b0
    return right, (x * 4 + z) * 4 + core * 2 + t


def fold(p):
    return jnp.sum(p.reshape(BLK // 8, 8, BLK), axis=0)


def total(acc):
    return jnp.sum(jnp.sum(acc, axis=0, keepdims=True), axis=1, keepdims=True)


def solve_kernel(ids, src_all, dst_all, lq_ref, rq_ref, psi_hbm, diag_hbm, *rest):
    groups = rest[:16]
    out_ref = rest[16]
    lbuf, rbuf, xv, hv, tv, gv, dv, vb, sems = rest[17:]
    site, op = ids[0], ids[1]
    place = (op // 4, op % 4, site % 2)

    copies = {}
    first = pltpu.make_async_copy(psi_hbm.at[0], vb, sems.at[16])
    first.start()
    for pick in range(2):
        for t in range(2):
            for side, buf in enumerate((lbuf, rbuf)):
                for half in range(2):
                    which = pick * 8 + half * 4 + t * 2 + side
                    begin = pick * 32 + t * 16 + half * 8
                    copy = pltpu.make_async_copy(
                        groups[which], buf.at[pl.ds(begin, 8)], sems.at[which]
                    )
                    copy.start()
                    copies.setdefault((pick, t), []).append(copy)
    second = pltpu.make_async_copy(diag_hbm.at[0], dv, sems.at[17])
    second.start()

    lq = lq_ref[...]
    lq_t = lq.T
    rq = rq_ref[...]
    rq_t = rq.T
    zero = jnp.zeros((8, BLK), F32)

    def over_blocks(step, count):
        return lax.fori_loop(0, NB, step, (zero,) * count)

    first.wait()

    def square(b, sums):
        v = vb[b].astype(F32)
        return (sums[0] + fold(v * v),)

    (norm,) = over_blocks(square, 1)
    scale = lax.rsqrt(total(norm) + 1e-12)

    def start(b, sums):
        v = vb[b].astype(F32) * scale
        xv[b] = v
        vb[b] = v.astype(BF16)
        hv[b] = jnp.zeros((BLK, BLK), F32)
        return sums

    over_blocks(start, 0)

    def term(k):
        right, which = term_slots(k, place)
        return k, right, src_all[which], dst_all[which]

    def apply_terms(terms, lefts, rights, acc):
        mids = []
        for (_, _, s, d), r in zip(terms, rights):
            mids.append((dot(vb[s], r).astype(BF16), dot_nt(vb[d], r).astype(BF16)))
        for (_, _, s, d), l, (f, b) in zip(terms, lefts, mids):
            acc[d] += dot(l, f)
            acc[s] += dot_tn(l, b)

    unroll = 4
    for pick in range(2):
        for t in range(2):
            for copy in copies[(pick, t)]:
                copy.wait()
            base = pick * 32 + t * 16

            def build(i, carry):
                terms = [term(base + i * unroll + u) for u in range(unroll)]
                temps = [
                    (dot(lbuf[k], lq).astype(BF16), dot(rbuf[r], rq_t).astype(BF16))
                    for k, r, _, _ in terms
                ]
                lefts = [dot(lq_t, lt).astype(BF16) for lt, _ in temps]
                rights = [dot(rq, rt).astype(BF16) for _, rt in temps]
                for (k, r, _, _), l, g in zip(terms, lefts, rights):
                    lbuf[k] = l
                    rbuf[r] = g
                apply_terms(terms, lefts, rights, hv)
                return carry

            lax.fori_loop(0, 16 // unroll, build, 0)

    second.wait()

    def finish_h(b, sums):
        x = xv[b]
        h = hv[b] + dv[b] * x
        hv[b] = h
        return (sums[0] + fold(x * h),)

    (theta_sum,) = over_blocks(finish_h, 1)
    theta = total(theta_sum)

    def correction(theta):
        def residual(b, sums):
            x = xv[b]
            t = (hv[b] - theta * x) / dv[b]
            tv[b] = t
            return (sums[0] + fold(x * t),)

        (along,) = over_blocks(residual, 1)
        along = total(along)

        def orthogonal(b, sums):
            t = tv[b] - along * xv[b]
            tv[b] = t
            return (sums[0] + fold(t * t),)

        (size,) = over_blocks(orthogonal, 1)
        return lax.rsqrt(total(size) + 1e-12)

    def rotation(theta, b, c):
        low = (c - theta) / 2 + jnp.sqrt(((theta - c) / 2) ** 2 + b * b)
        inv = 1.0 / jnp.sqrt(low * low + b * b)
        return low * inv, b * inv

    for step in range(ITERS - 1):
        scale_t = correction(theta)

        def unit(b, sums):
            t = tv[b] * scale_t
            tv[b] = t
            vb[b] = t.astype(BF16)
            gv[b] = dv[b] * t
            return sums

        over_blocks(unit, 0)

        def apply_step(i, carry):
            terms = [term(i * unroll + u) for u in range(unroll)]
            lefts = [lbuf[k] for k, _, _, _ in terms]
            rights = [rbuf[r] for _, r, _, _ in terms]
            apply_terms(terms, lefts, rights, gv)
            return carry

        lax.fori_loop(0, 64 // unroll, apply_step, 0)

        def couplings(b, sums):
            g = gv[b]
            return (sums[0] + fold(xv[b] * g), sums[1] + fold(tv[b] * g))

        cross, curve = over_blocks(couplings, 2)
        keep, move = rotation(theta, total(cross), total(curve))

        def update(b, sums):
            x = keep * xv[b] - move * tv[b]
            h = keep * hv[b] - move * gv[b]
            xv[b] = x
            hv[b] = h
            return (sums[0] + fold(x * h),)

        (theta_sum,) = over_blocks(update, 1)
        theta = total(theta_sum)

    scale_t = correction(theta)

    def last_unit(b, sums):
        t = tv[b] * scale_t
        tv[b] = t
        vb[b] = t.astype(BF16)
        return (sums[0] + fold(hv[b] * t), sums[1] + fold(dv[b] * t * t))

    cross, curve_diag = over_blocks(last_unit, 2)

    def last_step(i, acc):
        terms = [term(i * unroll + u) for u in range(unroll)]
        mids = [dot(vb[s], rbuf[r]).astype(BF16) for _, r, s, _ in terms]
        for (k, _, _, d), f in zip(terms, mids):
            acc = acc + fold(tv[d] * dot(lbuf[k], f))
        return acc

    curve_terms = lax.fori_loop(0, 64 // unroll, last_step, zero)
    curve = total(curve_diag) + 2.0 * total(curve_terms)
    keep, move = rotation(theta, total(cross), curve)
    amplitude = float(NB * BLK * BLK) ** 0.5
    out_ref[0, 0] = (keep * xv[op] - move * tv[op]) * amplitude


def solve(ids, src_all, dst_all, lq, rq, psi, diagonal, groups):
    smem = pl.BlockSpec(memory_space=pltpu.SMEM)
    vmem = pl.BlockSpec(memory_space=pltpu.VMEM)
    anywhere = pl.BlockSpec(memory_space=pl.ANY)
    full = (NB, BLK, BLK)
    return pl.pallas_call(
        solve_kernel,
        out_shape=jax.ShapeDtypeStruct((1, 1, BLK, BLK), F32),
        in_specs=[smem] * 3 + [vmem] * 2 + [anywhere] * 18,
        out_specs=vmem,
        scratch_shapes=[
            pltpu.VMEM((64, BLK, BLK), BF16),
            pltpu.VMEM((64, BLK, BLK), BF16),
            pltpu.VMEM(full, F32),
            pltpu.VMEM(full, F32),
            pltpu.VMEM(full, F32),
            pltpu.VMEM(full, F32),
            pltpu.VMEM(full, F32),
            pltpu.VMEM(full, BF16),
            pltpu.SemaphoreType.DMA((18,)),
        ],
        compiler_params=pltpu.CompilerParams(vmem_limit_bytes=56 * MIB),
        cost_estimate=pl.CostEstimate(
            flops=2 * 900 * BLK**3, bytes_accessed=24 * MIB, transcendentals=0
        ),
    )(ids, src_all, dst_all, lq, rq, psi, diagonal, *groups)


def body(psi, diagonal, left_step, right_step, left_env, right_env, src_block, dst_block):
    site = lax.axis_index("site")
    op = lax.axis_index("op")
    ids = jnp.stack([site, op]).astype(jnp.int32)
    core = site % 2
    left = lax.dynamic_slice_in_dim(left_env, 2 * core, 2, 0)
    right = lax.dynamic_slice_in_dim(right_env, 2 * core, 2, 0)
    held, last, held_across, last_across = gather_terms((left[0], right[0], left[1], right[1]))
    table = lax.all_gather(jnp.stack([src_block, dst_block]), "op")
    src_all = table[:, 0].reshape(-1)
    dst_all = table[:, 1].reshape(-1)
    lq, rq = transfers(ids, left_step, right_step)
    groups = held + last + held_across + last_across
    return solve(ids, src_all, dst_all, lq, rq, psi, diagonal, groups)


def solution(mesh):
    placed = (
        P("site", None, None, None),
        P("site", None, None, None),
        P("site", None, None),
        P("site", None, None),
        P("op", None, None),
        P("op", None, None),
        P("op"),
        P("op"),
    )
    return jax.shard_map(
        body, mesh=mesh, in_specs=placed, out_specs=P("site", "op", None, None), check_vma=False
    )
```

```python
import jax
import jax.numpy as jnp
from jax import lax
from jax.experimental import pallas as pl
from jax.experimental.pallas import tpu as pltpu
from jax.sharding import PartitionSpec as P

ITERS = 2
BLK = 256
NB = 16
TAIL = 16
ROWS = 2 * BLK + TAIL
BF16 = jnp.bfloat16
F32 = jnp.float32
I32 = jnp.int32
HIGH = lax.Precision.HIGHEST
MIB = 1 << 20
FULL = (NB, BLK, BLK)

XA, XB, ZA, ZB = (1, 0), (3, 0), (0, 1), (0, 3)
ORDERS = (
    ((XA, ZA, XB, ZB), (ZA, XB, ZB, XA)),
    ((XB, ZB, XA, ZA), (ZB, XA, ZA, XB)),
)

SMEM = pl.BlockSpec(memory_space=pltpu.SMEM)
VMEM = pl.BlockSpec(memory_space=pltpu.VMEM)
HBM = pl.BlockSpec(memory_space=pltpu.HBM)


def swap_op(value, part, stage):
    pairs = []
    for site in range(8):
        mx, mz = ORDERS[site % 2][part][stage]
        for x in range(4):
            for z in range(4):
                pairs.append((site * 16 + x * 4 + z, site * 16 + (x ^ mx) * 4 + (z ^ mz)))
    return lax.ppermute(value, ("site", "op"), pairs)


def swap_core(value):
    return lax.ppermute(value, "site", [(i, i ^ 1) for i in range(8)])


def dot(a, b):
    return jnp.dot(a, b, preferred_element_type=F32)


def dot_nt(a, b):
    return lax.dot_general(a, b, (((1,), (1,)), ((), ())), preferred_element_type=F32)


def dot_tn(a, b):
    return lax.dot_general(a, b, (((0,), (0,)), ((), ())), preferred_element_type=F32)


def dot_high(a, b):
    return jnp.dot(a, b, precision=HIGH, preferred_element_type=F32)


def identity():
    rows = lax.broadcasted_iota(I32, (BLK, BLK), 0)
    cols = lax.broadcasted_iota(I32, (BLK, BLK), 1)
    return jnp.where(rows == cols, 1.0, 0.0).astype(F32)


def pair_kernel(site_ref, own_ref, other_ref, out_ref):
    eye = identity()
    first = site_ref[0] % 2 == 0
    a = jnp.where(first, own_ref[0], other_ref[1])
    b = jnp.where(first, other_ref[0], own_ref[1])
    out_ref[...] = dot_high(eye + 0.3 * a, eye + 0.3 * b)


def pair_product(site, own, other):
    return pl.pallas_call(
        pair_kernel,
        out_shape=jax.ShapeDtypeStruct((BLK, BLK), F32),
        in_specs=[SMEM, VMEM, VMEM],
        out_specs=VMEM,
        cost_estimate=pl.CostEstimate(flops=12 * BLK**3, bytes_accessed=MIB, transcendentals=0),
    )(site, own, other)


def chain_kernel(site_ref, other_ref, m1, m2, m3, across, lq_ref, rq_ref):
    eye = identity()
    site = site_ref[0]
    core, y = site % 2, site // 2
    own = (m1, m2, m3)
    lefts, rights = [], []
    for k in range(3):
        left = jnp.where(core == 0, own[k][...], across[k])
        right = jnp.where(core == 0, across[k], own[k][...])
        lefts.append(jnp.where(y >= k + 1, left, eye))
        rights.append(jnp.where(y + k + 1 <= 3, right, eye))
    s_part = jnp.where(core == 1, eye + 0.3 * other_ref[0], eye)
    t_part = jnp.where(core == 0, eye + 0.3 * other_ref[1], eye)
    a = dot_high(lefts[2], lefts[1])
    b = dot_high(lefts[0], s_part)
    c = dot_high(t_part, rights[0])
    d = dot_high(rights[1], rights[2])
    lq_ref[...] = dot_high(a, b).astype(BF16)
    rq_ref[...] = dot_high(c, d).astype(BF16)


def chain_products(site, other, received, across):
    out = jax.ShapeDtypeStruct((BLK, BLK), BF16)
    return pl.pallas_call(
        chain_kernel,
        out_shape=(out, out),
        in_specs=[SMEM] + [VMEM] * 5,
        out_specs=(VMEM, VMEM),
        cost_estimate=pl.CostEstimate(flops=72 * BLK**3, bytes_accessed=2 * MIB, transcendentals=0),
    )(site, other, *received, across)


UNROLL = 4


def apply_terms(terms, lefts, rights, vb, acc):
    mids = []
    for (s, d), r in zip(terms, rights):
        mids.append((dot(vb[s], r).astype(BF16), dot_nt(vb[d], r).astype(BF16)))
    for (s, d), l, (f, b) in zip(terms, lefts, mids):
        acc[d] += dot(l, f)
        acc[s] += dot_tn(l, b)


def group_copies(group, lbuf, rbuf, tails, sems, g):
    spot = pl.ds(4 * g, 4)
    return (
        pltpu.make_async_copy(group.at[:, pl.ds(0, BLK)], lbuf.at[spot], sems.at[3 * g]),
        pltpu.make_async_copy(group.at[:, pl.ds(BLK, BLK)], rbuf.at[spot], sems.at[3 * g + 1]),
        pltpu.make_async_copy(group.at[:, pl.ds(2 * BLK, TAIL)], tails.at[spot], sems.at[3 * g + 2]),
    )


def load_terms(groups, lbuf, rbuf, tails, sems):
    copies = [
        group_copies(group, lbuf, rbuf, tails, sems, g) for g, group in enumerate(groups)
    ]
    for copy in [c[2] for c in copies] + [c for pair in copies for c in pair[:2]]:
        copy.start()


def read_blocks(groups, lbuf, rbuf, tails, sems, table_v, table, sem):
    for g, group in enumerate(groups):
        group_copies(group, lbuf, rbuf, tails, sems, g)[2].wait()
    table_v[...] = tails[:, 0, :128].astype(I32)
    move = pltpu.make_async_copy(table_v, table, sem)
    move.start()
    move.wait()


def build_and_apply(groups, lbuf, rbuf, tails, sems, table, lq_ref, rq_ref, vb, acc, done):
    lq = lq_ref[...]
    lq_t = lq.T
    rq = rq_ref[...]
    rq_t = rq.T

    def some(g, carry):
        left, right, _ = group_copies(groups[0], lbuf, rbuf, tails, sems, g)
        left.wait()
        right.wait()
        spots = [4 * g + u for u in range(4)]
        terms = [(table[k, 0], table[k, 1]) for k in spots]
        temps = [(dot(lbuf[k], lq).astype(BF16), dot(rbuf[k], rq_t).astype(BF16)) for k in spots]
        lefts = [dot(lq_t, lt).astype(BF16) for lt, _ in temps]
        rights = [dot(rq, rt).astype(BF16) for _, rt in temps]
        for k, l, r in zip(spots, lefts, rights):
            lbuf[k] = l
            rbuf[k] = r
        done(g)
        apply_terms(terms, lefts, rights, vb, acc)
        return carry

    lax.fori_loop(0, len(groups), some, 0)


def part_kernel(count, carried, lq_ref, rq_ref, vb_hbm, *rest):
    groups, rest = rest[:count], rest[count:]
    if carried:
        h_in, rest = rest[0], rest[1:]
    left_out, right_out, table_out, h_out = rest[:4]
    lbuf, rbuf, tails, table_v, table, vb, hv, sems, out_sems = rest[4:]
    load_terms(groups, lbuf, rbuf, tails, sems)
    start = pltpu.make_async_copy(vb_hbm, vb, sems.at[3 * count])
    start.start()
    if carried:
        before = pltpu.make_async_copy(h_in, hv, sems.at[3 * count + 1])
        before.start()
    else:
        def clear(b, carry):
            hv[b] = jnp.zeros((BLK, BLK), F32)
            return carry

        lax.fori_loop(0, NB, clear, 0)
    read_blocks(groups, lbuf, rbuf, tails, sems, table_v, table, sems.at[3 * count + 2])
    table_copy = pltpu.make_async_copy(table_v, table_out, out_sems.at[2 * count + 1])
    table_copy.start()

    def out_copies(g):
        spot = pl.ds(4 * g, 4)
        return (
            pltpu.make_async_copy(lbuf.at[spot], left_out.at[spot], out_sems.at[2 * g]),
            pltpu.make_async_copy(rbuf.at[spot], right_out.at[spot], out_sems.at[2 * g + 1]),
        )

    def done(g):
        for copy in out_copies(g):
            copy.start()

    start.wait()
    if carried:
        before.wait()
    build_and_apply(groups, lbuf, rbuf, tails, sems, table, lq_ref, rq_ref, vb, hv, done)
    last = pltpu.make_async_copy(hv, h_out, out_sems.at[2 * count])
    last.start()
    table_copy.wait()
    for g in range(count):
        for copy in out_copies(g):
            copy.wait()
    last.wait()


def part(groups, lq, rq, vb, h_in):
    count = len(groups)
    terms = 4 * count
    carried = h_in is not None

    def kernel(*refs):
        part_kernel(count, carried, *refs)

    env = jax.ShapeDtypeStruct((terms, BLK, BLK), BF16)
    return pl.pallas_call(
        kernel,
        out_shape=(
            env,
            env,
            jax.ShapeDtypeStruct((terms, 128), I32),
            jax.ShapeDtypeStruct(FULL, F32),
        ),
        in_specs=[VMEM, VMEM] + [HBM] * (1 + count + carried),
        out_specs=(HBM,) * 4,
        scratch_shapes=[
            pltpu.VMEM((terms, BLK, BLK), BF16),
            pltpu.VMEM((terms, BLK, BLK), BF16),
            pltpu.VMEM((terms, TAIL, BLK), BF16),
            pltpu.VMEM((terms, 128), I32),
            pltpu.SMEM((terms, 128), I32),
            pltpu.VMEM(FULL, BF16),
            pltpu.VMEM(FULL, F32),
            pltpu.SemaphoreType.DMA((3 * count + 3,)),
            pltpu.SemaphoreType.DMA((2 * count + 2,)),
        ],
        compiler_params=pltpu.CompilerParams(vmem_limit_bytes=56 * MIB),
        cost_estimate=pl.CostEstimate(
            flops=terms * 16 * BLK**3, bytes_accessed=terms * 8 * BLK * BLK, transcendentals=0
        ),
    )(lq, rq, vb, *groups, *((h_in,) if carried else ()))


def fold(p):
    return jnp.sum(p.reshape(BLK // 8, 8, BLK), axis=0)


def total(acc):
    return jnp.sum(jnp.sum(acc, axis=0, keepdims=True), axis=1, keepdims=True)


def solve_kernel(count, sizes, ids, lq_ref, rq_ref, x_hbm, diag_hbm, vb_hbm, h_hbm, *rest):
    tables, rest = rest[: len(sizes)], rest[len(sizes):]
    envs, rest = rest[: 2 * len(sizes)], rest[2 * len(sizes):]
    groups, rest = rest[:count], rest[count:]
    out_ref = rest[0]
    lbuf, rbuf, tails, table_v, table, xv, hv, tv, gv, dv, vb, sems, in_sems = rest[1:]
    op = ids[1]
    zero = jnp.zeros((8, BLK), F32)

    def over_blocks(step, sums):
        return lax.fori_loop(0, NB, step, (zero,) * sums)

    load_terms(groups, lbuf, rbuf, tails, sems)
    vectors = [
        pltpu.make_async_copy(source, target, in_sems.at[i])
        for i, (source, target) in enumerate(
            ((vb_hbm, vb), (h_hbm, hv), (x_hbm, xv), (diag_hbm.at[0], dv))
        )
    ]
    for copy in vectors:
        copy.start()
    built = []
    begin = 4 * count
    for i, size in enumerate(sizes):
        spot = pl.ds(begin, size)
        for j, (source, target) in enumerate(
            ((envs[2 * i], lbuf), (envs[2 * i + 1], rbuf), (tables[i], table))
        ):
            copy = pltpu.make_async_copy(source, target.at[spot], in_sems.at[4 + 3 * i + j])
            copy.start()
            built.append(copy)
        begin += size

    read_blocks(
        groups, lbuf, rbuf, tails, sems, table_v, table.at[pl.ds(0, 4 * count)], sems.at[3 * count]
    )
    vectors[0].wait()
    vectors[1].wait()
    build_and_apply(
        groups, lbuf, rbuf, tails, sems, table, lq_ref, rq_ref, vb, hv, lambda g: None
    )
    vectors[2].wait()
    vectors[3].wait()

    def finish_h(b, sums):
        x = xv[b]
        h = hv[b] + dv[b] * x
        hv[b] = h
        return (sums[0] + fold(x * h),)

    (theta_sum,) = over_blocks(finish_h, 1)
    theta = total(theta_sum)

    def correction(theta):
        def residual(b, sums):
            x = xv[b]
            t = (hv[b] - theta * x) / dv[b]
            tv[b] = t
            return (sums[0] + fold(x * t),)

        (along,) = over_blocks(residual, 1)
        along = total(along)

        def orthogonal(b, sums):
            t = tv[b] - along * xv[b]
            tv[b] = t
            return (sums[0] + fold(t * t),)

        (size,) = over_blocks(orthogonal, 1)
        return lax.rsqrt(total(size) + 1e-12)

    def rotation(theta, b, c):
        low = (c - theta) / 2 + jnp.sqrt(((theta - c) / 2) ** 2 + b * b)
        inv = 1.0 / jnp.sqrt(low * low + b * b)
        return low * inv, b * inv

    def over_terms(step, value):
        def some(i, value):
            spots = [i * UNROLL + u for u in range(UNROLL)]
            return step([(table[k, 0], table[k, 1]) for k in spots], spots, value)

        return lax.fori_loop(0, 64 // UNROLL, some, value)

    for step in range(ITERS - 1):
        scale_t = correction(theta)

        def unit(b, sums):
            t = tv[b] * scale_t
            tv[b] = t
            vb[b] = t.astype(BF16)
            gv[b] = dv[b] * t
            return sums

        over_blocks(unit, 0)
        if step == 0:
            for copy in built:
                copy.wait()

        def apply_step(terms, spots, value):
            apply_terms(terms, [lbuf[k] for k in spots], [rbuf[k] for k in spots], vb, gv)
            return value

        over_terms(apply_step, 0)

        def couplings(b, sums):
            g = gv[b]
            return (sums[0] + fold(xv[b] * g), sums[1] + fold(tv[b] * g))

        cross, curve = over_blocks(couplings, 2)
        keep, move = rotation(theta, total(cross), total(curve))

        def update(b, sums):
            x = keep * xv[b] - move * tv[b]
            h = keep * hv[b] - move * gv[b]
            xv[b] = x
            hv[b] = h
            return (sums[0] + fold(x * h),)

        (theta_sum,) = over_blocks(update, 1)
        theta = total(theta_sum)

    scale_t = correction(theta)

    def last_unit(b, sums):
        t = tv[b] * scale_t
        tv[b] = t
        vb[b] = t.astype(BF16)
        return (sums[0] + fold(hv[b] * t), sums[1] + fold(dv[b] * t * t))

    cross, curve_diag = over_blocks(last_unit, 2)

    def last_step(terms, spots, acc):
        mids = [dot(vb[s], rbuf[k]).astype(BF16) for (s, _), k in zip(terms, spots)]
        for (_, d), k, f in zip(terms, spots, mids):
            acc = acc + fold(tv[d] * dot(lbuf[k], f))
        return acc

    curve_terms = over_terms(last_step, zero)
    curve = total(curve_diag) + 2.0 * total(curve_terms)
    keep, move = rotation(theta, total(cross), curve)
    amplitude = float(NB * BLK * BLK) ** 0.5
    out_ref[0, 0] = (keep * xv[op] - move * tv[op]) * amplitude


def solve(ids, parts, lq, rq, x, diagonal, vb, h, groups):
    count = len(groups)
    sizes = tuple(p[0].shape[0] for p in parts)

    def kernel(*refs):
        solve_kernel(count, sizes, *refs)

    return pl.pallas_call(
        kernel,
        out_shape=jax.ShapeDtypeStruct((1, 1, BLK, BLK), F32),
        in_specs=[SMEM, VMEM, VMEM] + [HBM] * (4 + 3 * len(sizes) + count),
        out_specs=VMEM,
        scratch_shapes=[
            pltpu.VMEM((64, BLK, BLK), BF16),
            pltpu.VMEM((64, BLK, BLK), BF16),
            pltpu.VMEM((4 * count, TAIL, BLK), BF16),
            pltpu.VMEM((4 * count, 128), I32),
            pltpu.SMEM((64, 128), I32),
            pltpu.VMEM(FULL, F32),
            pltpu.VMEM(FULL, F32),
            pltpu.VMEM(FULL, F32),
            pltpu.VMEM(FULL, F32),
            pltpu.VMEM(FULL, F32),
            pltpu.VMEM(FULL, BF16),
            pltpu.SemaphoreType.DMA((3 * count + 1,)),
            pltpu.SemaphoreType.DMA((4 + 3 * len(sizes),)),
        ],
        compiler_params=pltpu.CompilerParams(vmem_limit_bytes=56 * MIB),
        cost_estimate=pl.CostEstimate(
            flops=2 * 500 * BLK**3, bytes_accessed=24 * MIB, transcendentals=0
        ),
    )(
        ids,
        lq,
        rq,
        x,
        diagonal,
        vb,
        h,
        *[p[2] for p in parts],
        *[env for p in parts for env in p[:2]],
        *groups,
    )


def start_kernel(psi_ref, x_hbm, vb_hbm, xv, vb, sems):
    def square(b, acc):
        v = psi_ref[0, b].astype(F32)
        return acc + fold(v * v)

    norm = lax.fori_loop(0, NB, square, jnp.zeros((8, BLK), F32))
    scale = lax.rsqrt(total(norm) + 1e-12)

    def unit(b, carry):
        v = psi_ref[0, b].astype(F32) * scale
        xv[b] = v
        vb[b] = v.astype(BF16)
        return carry

    lax.fori_loop(0, NB, unit, 0)
    copies = (
        pltpu.make_async_copy(xv, x_hbm, sems.at[0]),
        pltpu.make_async_copy(vb, vb_hbm, sems.at[1]),
    )
    for copy in copies:
        copy.start()
    for copy in copies:
        copy.wait()


def start_vector(psi):
    return pl.pallas_call(
        start_kernel,
        out_shape=(jax.ShapeDtypeStruct(FULL, F32), jax.ShapeDtypeStruct(FULL, BF16)),
        in_specs=[VMEM],
        out_specs=(HBM, HBM),
        scratch_shapes=[
            pltpu.VMEM(FULL, F32),
            pltpu.VMEM(FULL, BF16),
            pltpu.SemaphoreType.DMA((2,)),
        ],
        compiler_params=pltpu.CompilerParams(vmem_limit_bytes=20 * MIB),
        cost_estimate=pl.CostEstimate(flops=8 * MIB, bytes_accessed=12 * MIB, transcendentals=0),
    )(psi)


def after(values, marks):
    return lax.optimization_barrier((tuple(values), tuple(marks)))[0]


def body(psi, diagonal, left_step, right_step, left_env, right_env, src_block, dst_block):
    site = lax.axis_index("site")
    op = lax.axis_index("op")
    ids = jnp.stack([site, op]).astype(I32)
    core = site % 2

    blocks = jnp.stack([src_block, dst_block], 1).astype(BF16)
    tails = jnp.pad(blocks[:, None, :], ((0, 0), (0, TAIL - 1), (0, BLK - 2)))
    whole = jnp.concatenate([left_env, right_env, tails], 1)
    mine = lax.dynamic_slice_in_dim(whole, 2 * core, 2, 0)
    parts = (mine[:1], mine[1:])

    steps = jnp.concatenate([left_step, right_step], 0)
    first = [swap_op(p, i, 0) for i, p in enumerate(parts)]
    other = swap_core(steps)
    product = pair_product(ids, steps, other)

    two = [jnp.concatenate(pair, 0) for pair in zip(parts, first)]
    two, product = lax.optimization_barrier((two, product))
    second = [swap_op(p, i, 1) for i, p in enumerate(two)]
    received = []
    for k in (1, 2, 3):
        pairs = [(2 * y, 2 * (y + k)) for y in range(4 - k)]
        pairs += [(2 * y + 1, 2 * (y - k) + 1) for y in range(k, 4)]
        received.append(lax.ppermute(product, "site", pairs))

    four = [jnp.concatenate(pair, 0) for pair in zip(two, second)]
    third = [swap_op(p, i, 2) for i, p in enumerate(four)]
    received, (psi,) = lax.optimization_barrier((received, after((psi,), four)))
    across = swap_core(jnp.stack(received))
    x, vb = start_vector(psi)
    lq, rq = chain_products(ids, other, received, across)
    four, (lq, rq, vb) = lax.optimization_barrier((four, (lq, rq, vb)))
    old = [swap_op(p, i, 3) for i, p in enumerate(four)]
    new = [swap_op(p, i, 3) for i, p in enumerate(third)]

    def both(groups):
        return list(groups) + [swap_core(g) for g in groups]

    built = [part(both(four), lq, rq, vb, None)]
    old = after(old, built[-1][3:])
    built.append(part(both(third), lq, rq, vb, built[-1][3]))
    new = after(new, built[-1][3:])
    return solve(ids, built, lq, rq, x, diagonal, vb, built[-1][3], both(old) + both(new))


def solution(mesh):
    placed = (
        P("site", None, None, None),
        P("site", None, None, None),
        P("site", None, None),
        P("site", None, None),
        P("op", None, None),
        P("op", None, None),
        P("op"),
        P("op"),
    )
    return jax.shard_map(
        body, mesh=mesh, in_specs=placed, out_specs=P("site", "op", None, None), check_vma=False
    )
```

```python
import functools

import jax
import jax.numpy as jnp
from jax import lax
from jax.experimental import pallas as pl
from jax.experimental.pallas import tpu as pltpu
from jax.sharding import PartitionSpec as P

ITERS = 2
BLK = 256
NB = 16
TAIL = 16
ROWS = 2 * BLK + TAIL
BF16 = jnp.bfloat16
F32 = jnp.float32
I32 = jnp.int32
HIGH = lax.Precision.HIGHEST
MIB = 1 << 20
FULL = (NB, BLK, BLK)

XA, XB, ZA, ZB = (1, 0), (3, 0), (0, 1), (0, 3)
ORDERS = (
    ((XA, ZA, XB, ZB), (ZA, XB, ZB, XA)),
    ((XB, ZB, XA, ZA), (ZB, XA, ZA, XB)),
)

LIGHT = pl.CostEstimate(flops=1, bytes_accessed=1, transcendentals=0)
SMEM = pl.BlockSpec(memory_space=pltpu.SMEM)
VMEM = pl.BlockSpec(memory_space=pltpu.VMEM)
HBM = pl.BlockSpec(memory_space=pl.ANY)


def swap_op(value, part, stage):
    pairs = []
    for site in range(8):
        mx, mz = ORDERS[site % 2][part][stage]
        for x in range(4):
            for z in range(4):
                pairs.append((site * 16 + x * 4 + z, site * 16 + (x ^ mx) * 4 + (z ^ mz)))
    return lax.ppermute(value, ("site", "op"), pairs)


def swap_core(value):
    return lax.ppermute(value, "site", [(i, i ^ 1) for i in range(8)])


def dot(a, b):
    return jnp.dot(a, b, preferred_element_type=F32)


def dot_nt(a, b):
    return lax.dot_general(a, b, (((1,), (1,)), ((), ())), preferred_element_type=F32)


def dot_tn(a, b):
    return lax.dot_general(a, b, (((0,), (0,)), ((), ())), preferred_element_type=F32)


def dot_high(a, b):
    return jnp.dot(a, b, precision=HIGH, preferred_element_type=F32)


def identity():
    rows = lax.broadcasted_iota(I32, (BLK, BLK), 0)
    cols = lax.broadcasted_iota(I32, (BLK, BLK), 1)
    return jnp.where(rows == cols, 1.0, 0.0).astype(F32)


def pair_kernel(site_ref, own_left, own_right, other_left, other_right, out_ref):
    eye = identity()
    first = site_ref[0] % 2 == 0
    a = jnp.where(first, own_left[...], other_right[...])
    b = jnp.where(first, other_left[...], own_right[...])
    out_ref[...] = dot_high(eye + 0.3 * a, eye + 0.3 * b)


def pair_product(site, own, other):
    return pl.pallas_call(
        pair_kernel,
        out_shape=jax.ShapeDtypeStruct((BLK, BLK), F32),
        in_specs=[SMEM] + [VMEM] * 4,
        out_specs=VMEM,
        cost_estimate=LIGHT,
    )(site, *own, *other)


def chain_kernel(site_ref, other_left, other_right, m1, m2, m3, n1, n2, n3, lq_ref, rq_ref):
    eye = identity()
    site = site_ref[0]
    core, y = site % 2, site // 2
    own, across = (m1, m2, m3), (n1, n2, n3)
    lefts, rights = [], []
    for k in range(3):
        left = jnp.where(core == 0, own[k][...], across[k][...])
        right = jnp.where(core == 0, across[k][...], own[k][...])
        lefts.append(jnp.where(y >= k + 1, left, eye))
        rights.append(jnp.where(y + k + 1 <= 3, right, eye))
    s_part = jnp.where(core == 1, eye + 0.3 * other_left[...], eye)
    t_part = jnp.where(core == 0, eye + 0.3 * other_right[...], eye)
    a = dot_high(lefts[2], lefts[1])
    b = dot_high(lefts[0], s_part)
    c = dot_high(t_part, rights[0])
    d = dot_high(rights[1], rights[2])
    lq_ref[...] = dot_high(a, b).astype(BF16)
    rq_ref[...] = dot_high(c, d).astype(BF16)


def chain_products(site, other, received, across):
    out = jax.ShapeDtypeStruct((BLK, BLK), BF16)
    return pl.pallas_call(
        chain_kernel,
        out_shape=(out, out),
        in_specs=[SMEM] + [VMEM] * 8,
        out_specs=(VMEM, VMEM),
        cost_estimate=LIGHT,
    )(site, *other, *received, *across)


UNROLL = 4


def apply_terms(terms, lefts, rights, vb, acc):
    mids = []
    for (s, d), r in zip(terms, rights):
        mids.append((dot(vb[s], r).astype(BF16), dot_nt(vb[d], r).astype(BF16)))
    for (s, d), l, (f, b) in zip(terms, lefts, mids):
        acc[d] += dot(l, f)
        acc[s] += dot_tn(l, b)


def group_copies(group, lbuf, rbuf, tails, sems, g):
    spot = pl.ds(4 * g, 4)
    return (
        pltpu.make_async_copy(group.at[:, pl.ds(0, BLK)], lbuf.at[spot], sems.at[3 * g]),
        pltpu.make_async_copy(group.at[:, pl.ds(BLK, BLK)], rbuf.at[spot], sems.at[3 * g + 1]),
        pltpu.make_async_copy(group.at[:, pl.ds(2 * BLK, TAIL)], tails.at[spot], sems.at[3 * g + 2]),
    )


def load_terms(groups, lbuf, rbuf, tails, sems):
    copies = [
        group_copies(group, lbuf, rbuf, tails, sems, g) for g, group in enumerate(groups)
    ]
    for copy in [c[2] for c in copies] + [c for pair in copies for c in pair[:2]]:
        copy.start()


def read_blocks(groups, lbuf, rbuf, tails, sems, table_v, table, sem):
    for g, group in enumerate(groups):
        group_copies(group, lbuf, rbuf, tails, sems, g)[2].wait()
    table_v[...] = tails[:, 0, :128].astype(I32)
    move = pltpu.make_async_copy(table_v, table, sem)
    move.start()
    move.wait()


def build_and_apply(groups, lbuf, rbuf, tails, sems, table, lq_ref, rq_ref, vb, acc, done):
    lq = lq_ref[...]
    lq_t = lq.T
    rq = rq_ref[...]
    rq_t = rq.T

    def some(g, carry):
        left, right, _ = group_copies(groups[0], lbuf, rbuf, tails, sems, g)
        left.wait()
        right.wait()
        spots = [4 * g + u for u in range(4)]
        terms = [(table[k, 0], table[k, 1]) for k in spots]
        temps = [(dot(lbuf[k], lq).astype(BF16), dot(rbuf[k], rq_t).astype(BF16)) for k in spots]
        lefts = [dot(lq_t, lt).astype(BF16) for lt, _ in temps]
        rights = [dot(rq, rt).astype(BF16) for _, rt in temps]
        for k, l, r in zip(spots, lefts, rights):
            lbuf[k] = l
            rbuf[k] = r
        done(g)
        apply_terms(terms, lefts, rights, vb, acc)
        return carry

    lax.fori_loop(0, len(groups), some, 0)


def part_kernel(count, carried, lq_ref, rq_ref, vb_hbm, *rest):
    groups, rest = rest[:count], rest[count:]
    if carried:
        h_in, rest = rest[0], rest[1:]
    left_out, right_out, table_out, h_out = rest[:4]
    lbuf, rbuf, tails, table_v, table, vb, hv, sems, out_sems = rest[4:]
    start = pltpu.make_async_copy(vb_hbm, vb, sems.at[3 * count])
    start.start()
    if carried:
        before = pltpu.make_async_copy(h_in, hv, sems.at[3 * count + 1])
        before.start()
    load_terms(groups, lbuf, rbuf, tails, sems)
    if not carried:
        def clear(b, carry):
            hv[b] = jnp.zeros((BLK, BLK), F32)
            return carry

        lax.fori_loop(0, NB, clear, 0)
    read_blocks(groups, lbuf, rbuf, tails, sems, table_v, table, sems.at[3 * count + 2])
    table_copy = pltpu.make_async_copy(table_v, table_out, out_sems.at[2 * count + 1])
    table_copy.start()

    def out_copies(g):
        spot = pl.ds(4 * g, 4)
        return (
            pltpu.make_async_copy(lbuf.at[spot], left_out.at[spot], out_sems.at[2 * g]),
            pltpu.make_async_copy(rbuf.at[spot], right_out.at[spot], out_sems.at[2 * g + 1]),
        )

    def done(g):
        for copy in out_copies(g):
            copy.start()

    start.wait()
    if carried:
        before.wait()
    build_and_apply(groups, lbuf, rbuf, tails, sems, table, lq_ref, rq_ref, vb, hv, done)
    last = pltpu.make_async_copy(hv, h_out, out_sems.at[2 * count])
    last.start()
    table_copy.wait()
    for g in range(count):
        for copy in out_copies(g):
            copy.wait()
    last.wait()


def part(groups, lq, rq, vb, h_in):
    count = len(groups)
    terms = 4 * count
    carried = h_in is not None

    def kernel(*refs):
        part_kernel(count, carried, *refs)

    env = jax.ShapeDtypeStruct((terms, BLK, BLK), BF16)
    return pl.pallas_call(
        kernel,
        out_shape=(
            env,
            env,
            jax.ShapeDtypeStruct((terms, 128), I32),
            jax.ShapeDtypeStruct(FULL, F32),
        ),
        in_specs=[VMEM, VMEM] + [HBM] * (1 + count + carried),
        out_specs=(HBM,) * 4,
        scratch_shapes=[
            pltpu.VMEM((terms, BLK, BLK), BF16),
            pltpu.VMEM((terms, BLK, BLK), BF16),
            pltpu.VMEM((terms, TAIL, BLK), BF16),
            pltpu.VMEM((terms, 128), I32),
            pltpu.SMEM((terms, 128), I32),
            pltpu.VMEM(FULL, BF16),
            pltpu.VMEM(FULL, F32),
            pltpu.SemaphoreType.DMA((3 * count + 3,)),
            pltpu.SemaphoreType.DMA((2 * count + 2,)),
        ],
        compiler_params=pltpu.CompilerParams(vmem_limit_bytes=18 * MIB),
        cost_estimate=LIGHT,
    )(lq, rq, vb, *groups, *((h_in,) if carried else ()))


def fold(p):
    return jnp.sum(p.reshape(BLK // 8, 8, BLK), axis=0)


def total(acc):
    return jnp.sum(jnp.sum(acc, axis=0, keepdims=True), axis=1, keepdims=True)


def solve_kernel(count, sizes, ids, lq_ref, rq_ref, scale_ref, psi_hbm, diag_hbm, vb_hbm, h_hbm, *rest):
    tables, rest = rest[: len(sizes)], rest[len(sizes):]
    envs, rest = rest[: 2 * len(sizes)], rest[2 * len(sizes):]
    groups, rest = rest[:count], rest[count:]
    out_ref = rest[0]
    lbuf, rbuf, tails, table_v, table, xv, hv, tv, gv, dv, vb, psi, sems, in_sems = rest[1:]
    op = ids[1]
    zero = jnp.zeros((8, BLK), F32)

    def over_blocks(step, sums):
        return lax.fori_loop(0, NB, step, (zero,) * sums)

    vectors = [
        pltpu.make_async_copy(source, target, in_sems.at[i])
        for i, (source, target) in enumerate(
            ((vb_hbm, vb), (h_hbm, hv), (psi_hbm.at[0], psi), (diag_hbm.at[0], dv))
        )
    ]
    for copy in vectors[:2]:
        copy.start()
    load_terms(groups, lbuf, rbuf, tails, sems)
    for copy in vectors[2:]:
        copy.start()
    built = []
    begin = 4 * count
    for i, size in enumerate(sizes):
        spot = pl.ds(begin, size)
        for j, (source, target) in enumerate(
            ((envs[2 * i], lbuf), (envs[2 * i + 1], rbuf), (tables[i], table))
        ):
            copy = pltpu.make_async_copy(source, target.at[spot], in_sems.at[4 + 3 * i + j])
            copy.start()
            built.append(copy)
        begin += size

    read_blocks(
        groups, lbuf, rbuf, tails, sems, table_v, table.at[pl.ds(0, 4 * count)], sems.at[3 * count]
    )
    vectors[0].wait()
    vectors[1].wait()
    build_and_apply(
        groups, lbuf, rbuf, tails, sems, table, lq_ref, rq_ref, vb, hv, lambda g: None
    )
    vectors[2].wait()
    vectors[3].wait()

    start_scale = scale_ref[0:1, 0:1]

    def finish_h(b, sums):
        x = psi[b].astype(F32) * start_scale
        h = hv[b] + dv[b] * x
        xv[b] = x
        hv[b] = h
        return (sums[0] + fold(x * h),)

    (theta_sum,) = over_blocks(finish_h, 1)
    theta = total(theta_sum)

    def residual(b, sums):
        x = xv[b]
        t = (hv[b] - theta * x) / dv[b]
        tv[b] = t
        return (sums[0] + fold(x * t),)

    (along,) = over_blocks(residual, 1)

    def orthogonal(along, b, sums):
        t = tv[b] - along * xv[b]
        tv[b] = t
        return (sums[0] + fold(t * t),)

    def rotation(theta, b, c):
        low = (c - theta) / 2 + jnp.sqrt(((theta - c) / 2) ** 2 + b * b)
        inv = 1.0 / jnp.sqrt(low * low + b * b)
        return low * inv, b * inv

    def over_terms(step, value, unroll=UNROLL):
        def some(i, value):
            spots = [i * unroll + u for u in range(unroll)]
            return step([(table[k, 0], table[k, 1]) for k in spots], spots, value)

        return lax.fori_loop(0, 64 // unroll, some, value)

    for step in range(ITERS - 1):
        (size,) = over_blocks(functools.partial(orthogonal, total(along)), 1)
        scale_t = lax.rsqrt(total(size) + 1e-12)

        def unit(b, sums):
            t = tv[b] * scale_t
            tv[b] = t
            vb[b] = t.astype(BF16)
            gv[b] = dv[b] * t
            return sums

        over_blocks(unit, 0)
        if step == 0:
            for copy in built:
                copy.wait()

        def apply_step(terms, spots, value):
            apply_terms(terms, [lbuf[k] for k in spots], [rbuf[k] for k in spots], vb, gv)
            return value

        over_terms(apply_step, 0)

        def couplings(b, sums):
            g = gv[b]
            t = tv[b]
            return (sums[0] + fold(xv[b] * g), sums[1] + fold(t * g), sums[2] + fold(t * hv[b]))

        sums = over_blocks(couplings, 3)
        cross, curve, back = (total(v) for v in sums)
        keep, move = rotation(theta, cross, curve)
        theta = keep * keep * theta - keep * move * (cross + back) + move * move * curve

        def turn(keep, move, theta, b, sums):
            x = keep * xv[b] - move * tv[b]
            h = keep * hv[b] - move * gv[b]
            xv[b] = x
            hv[b] = h
            t = (h - theta * x) / dv[b]
            tv[b] = t
            return (sums[0] + fold(x * t),)

        (along,) = over_blocks(functools.partial(turn, keep, move, theta), 1)

    (size,) = over_blocks(functools.partial(orthogonal, total(along)), 1)
    scale_t = lax.rsqrt(total(size) + 1e-12)

    def last_unit(b, sums):
        t = tv[b] * scale_t
        tv[b] = t
        vb[b] = t.astype(BF16)
        return (sums[0] + fold(hv[b] * t), sums[1] + fold(dv[b] * t * t))

    cross, curve_diag = over_blocks(last_unit, 2)

    def last_step(terms, spots, acc):
        mids = [dot(vb[s], rbuf[k]).astype(BF16) for (s, _), k in zip(terms, spots)]
        for (_, d), k, f in zip(terms, spots, mids):
            acc = acc + fold(tv[d] * dot(lbuf[k], f))
        return acc

    curve_terms = over_terms(last_step, zero, 2 * UNROLL)
    curve = total(curve_diag) + 2.0 * total(curve_terms)
    keep, move = rotation(theta, total(cross), curve)
    amplitude = float(NB * BLK * BLK) ** 0.5
    out_ref[0, 0] = (keep * xv[op] - move * tv[op]) * amplitude


def solve(ids, parts, lq, rq, scale, psi, diagonal, vb, h, groups):
    count = len(groups)
    sizes = tuple(p[0].shape[0] for p in parts)

    def kernel(*refs):
        solve_kernel(count, sizes, *refs)

    return pl.pallas_call(
        kernel,
        out_shape=jax.ShapeDtypeStruct((1, 1, BLK, BLK), F32),
        in_specs=[SMEM] + [VMEM] * 3 + [HBM] * (4 + 3 * len(sizes) + count),
        out_specs=VMEM,
        scratch_shapes=[
            pltpu.VMEM((64, BLK, BLK), BF16),
            pltpu.VMEM((64, BLK, BLK), BF16),
            pltpu.VMEM((4 * count, TAIL, BLK), BF16),
            pltpu.VMEM((4 * count, 128), I32),
            pltpu.SMEM((64, 128), I32),
            pltpu.VMEM(FULL, F32),
            pltpu.VMEM(FULL, F32),
            pltpu.VMEM(FULL, F32),
            pltpu.VMEM(FULL, F32),
            pltpu.VMEM(FULL, F32),
            pltpu.VMEM(FULL, BF16),
            pltpu.VMEM(FULL, BF16),
            pltpu.SemaphoreType.DMA((3 * count + 1,)),
            pltpu.SemaphoreType.DMA((4 + 3 * len(sizes),)),
        ],
        compiler_params=pltpu.CompilerParams(vmem_limit_bytes=46 * MIB),
        cost_estimate=LIGHT,
    )(
        ids,
        lq,
        rq,
        scale,
        psi,
        diagonal,
        vb,
        h,
        *[p[2] for p in parts],
        *[env for p in parts for env in p[:2]],
        *groups,
    )


def start_kernel(psi_ref, vb_ref, scale_ref):
    def square(b, acc):
        v = psi_ref[0, b].astype(F32)
        return acc + fold(v * v)

    norm = lax.fori_loop(0, NB, square, jnp.zeros((8, BLK), F32))
    scale = lax.rsqrt(total(norm) + 1e-12)
    scale_ref[...] = jnp.broadcast_to(scale, (8, 128))

    def unit(b, carry):
        vb_ref[b] = (psi_ref[0, b].astype(F32) * scale).astype(BF16)
        return carry

    lax.fori_loop(0, NB, unit, 0)


def start_vector(psi):
    return pl.pallas_call(
        start_kernel,
        out_shape=(
            jax.ShapeDtypeStruct(FULL, BF16),
            jax.ShapeDtypeStruct((8, 128), F32),
        ),
        in_specs=[VMEM],
        out_specs=(VMEM, VMEM),
        compiler_params=pltpu.CompilerParams(vmem_limit_bytes=8 * MIB),
        cost_estimate=LIGHT,
    )(psi)


def after(values, marks):
    return lax.optimization_barrier((tuple(values), tuple(marks)))[0]


def body(psi, diagonal, left_step, right_step, left_env, right_env, src_block, dst_block):
    site = lax.axis_index("site")
    op = lax.axis_index("op")
    ids = jnp.stack([site, op]).astype(I32)
    core = site % 2

    blocks = jnp.stack([src_block, dst_block], 1).astype(BF16)
    tails = jnp.pad(blocks[:, None, :], ((0, 0), (0, TAIL - 1), (0, BLK - 2)))
    whole = jnp.concatenate([left_env, right_env, tails], 1)
    mine = lax.dynamic_slice_in_dim(whole, 2 * core, 2, 0)
    parts = (mine[:1], mine[1:])

    first = [swap_op(p, i, 0) for i, p in enumerate(parts)]
    steps = (left_step[0], right_step[0])
    other = tuple(swap_core(step) for step in steps)
    product = pair_product(ids, steps, other)

    two = [jnp.concatenate(pair, 0) for pair in zip(parts, first)]
    two, product = lax.optimization_barrier((two, product))
    second = [swap_op(p, i, 1) for i, p in enumerate(two)]
    received = []
    for k in (1, 2, 3):
        pairs = [(2 * y, 2 * (y + k)) for y in range(4 - k)]
        pairs += [(2 * y + 1, 2 * (y - k) + 1) for y in range(k, 4)]
        received.append(lax.ppermute(product, "site", pairs))
    across = [swap_core(r) for r in received]

    four = [jnp.concatenate(pair, 0) for pair in zip(two, second)]
    third = [swap_op(p, i, 2) for i, p in enumerate(four)]
    psi, received, across = after((psi, tuple(received), tuple(across)), four)
    vb, scale = start_vector(psi)
    lq, rq = chain_products(ids, other, received, across)
    old = [swap_op(p, i, 3) for i, p in enumerate(four)]

    def both(groups):
        return list(groups) + [swap_core(g) for g in groups]

    built = [part(both(four), lq, rq, vb, None)]
    third = after(third, built[-1][3:])
    new = [swap_op(p, i, 3) for i, p in enumerate(third)]
    old = after(old, built[-1][3:])
    built.append(part(both(third), lq, rq, vb, built[-1][3]))
    new = after(new, built[-1][3:])
    return solve(ids, built, lq, rq, scale, psi, diagonal, vb, built[-1][3], both(old) + both(new))


def solution(mesh):
    placed = (
        P("site", None, None, None),
        P("site", None, None, None),
        P("site", None, None),
        P("site", None, None),
        P("op", None, None),
        P("op", None, None),
        P("op"),
        P("op"),
    )
    return jax.shard_map(
        body, mesh=mesh, in_specs=placed, out_specs=P("site", "op", None, None), check_vma=False
    )
```

```python
import functools

import jax
import jax.numpy as jnp
from jax import lax
from jax.experimental import pallas as pl
from jax.experimental.pallas import tpu as pltpu
from jax.sharding import PartitionSpec as P

ITERS = 2
BLK = 256
NB = 16
TAIL = 16
ROWS = 2 * BLK + TAIL
BF16 = jnp.bfloat16
F32 = jnp.float32
I32 = jnp.int32
HIGH = lax.Precision.HIGHEST
MIB = 1 << 20
FULL = (NB, BLK, BLK)

XA, XB, ZA, ZB = (1, 0), (3, 0), (0, 1), (0, 3)
ORDERS = (
    ((XA, ZA, XB, ZB), (ZA, XB, ZB, XA)),
    ((XB, ZB, XA, ZA), (ZB, XA, ZA, XB)),
)

LIGHT = pl.CostEstimate(flops=1, bytes_accessed=1, transcendentals=0)
SMEM = pl.BlockSpec(memory_space=pltpu.SMEM)
VMEM = pl.BlockSpec(memory_space=pltpu.VMEM)
HBM = pl.BlockSpec(memory_space=pl.ANY)


def swap_op(value, part, stage):
    pairs = []
    for site in range(8):
        mx, mz = ORDERS[site % 2][part][stage]
        for x in range(4):
            for z in range(4):
                pairs.append((site * 16 + x * 4 + z, site * 16 + (x ^ mx) * 4 + (z ^ mz)))
    return lax.ppermute(value, ("site", "op"), pairs)


def swap_core(value):
    return lax.ppermute(value, "site", [(i, i ^ 1) for i in range(8)])


def dot(a, b):
    return jnp.dot(a, b, preferred_element_type=F32)


def dot_nt(a, b):
    return lax.dot_general(a, b, (((1,), (1,)), ((), ())), preferred_element_type=F32)


def dot_tn(a, b):
    return lax.dot_general(a, b, (((0,), (0,)), ((), ())), preferred_element_type=F32)


def dot_high(a, b):
    return jnp.dot(a, b, precision=HIGH, preferred_element_type=F32)


def identity():
    rows = lax.broadcasted_iota(I32, (BLK, BLK), 0)
    cols = lax.broadcasted_iota(I32, (BLK, BLK), 1)
    return jnp.where(rows == cols, 1.0, 0.0).astype(F32)


def pair_kernel(site_ref, own_left, own_right, other_left, other_right, out_ref):
    eye = identity()
    first = site_ref[0] % 2 == 0
    a = jnp.where(first, own_left[...], other_right[...])
    b = jnp.where(first, other_left[...], own_right[...])
    out_ref[...] = dot_high(eye + 0.3 * a, eye + 0.3 * b)


def pair_product(site, own, other):
    return pl.pallas_call(
        pair_kernel,
        out_shape=jax.ShapeDtypeStruct((BLK, BLK), F32),
        in_specs=[SMEM] + [VMEM] * 4,
        out_specs=VMEM,
        cost_estimate=LIGHT,
    )(site, *own, *other)


def chain_kernel(site_ref, other_left, other_right, m1, m2, m3, n1, n2, n3, lq_ref, rq_ref):
    eye = identity()
    site = site_ref[0]
    core, y = site % 2, site // 2
    own, across = (m1, m2, m3), (n1, n2, n3)
    lefts, rights = [], []
    for k in range(3):
        left = jnp.where(core == 0, own[k][...], across[k][...])
        right = jnp.where(core == 0, across[k][...], own[k][...])
        lefts.append(jnp.where(y >= k + 1, left, eye))
        rights.append(jnp.where(y + k + 1 <= 3, right, eye))
    s_part = jnp.where(core == 1, eye + 0.3 * other_left[...], eye)
    t_part = jnp.where(core == 0, eye + 0.3 * other_right[...], eye)
    a = dot_high(lefts[2], lefts[1])
    b = dot_high(lefts[0], s_part)
    c = dot_high(t_part, rights[0])
    d = dot_high(rights[1], rights[2])
    lq_ref[...] = dot_high(a, b).astype(BF16)
    rq_ref[...] = dot_high(c, d).astype(BF16)


def chain_products(site, other, received, across):
    out = jax.ShapeDtypeStruct((BLK, BLK), BF16)
    return pl.pallas_call(
        chain_kernel,
        out_shape=(out, out),
        in_specs=[SMEM] + [VMEM] * 8,
        out_specs=(VMEM, VMEM),
        cost_estimate=LIGHT,
    )(site, *other, *received, *across)


UNROLL = 4


def apply_terms(terms, lefts, rights, vb, acc):
    mids = []
    for (s, d), r in zip(terms, rights):
        mids.append((dot(vb[s], r).astype(BF16), dot_nt(vb[d], r).astype(BF16)))
    for (s, d), l, (f, b) in zip(terms, lefts, mids):
        acc[d] += dot(l, f)
        acc[s] += dot_tn(l, b)


def group_copies(group, lbuf, rbuf, tails, sems, g):
    spot = pl.ds(4 * g, 4)
    return (
        pltpu.make_async_copy(group.at[:, pl.ds(0, BLK)], lbuf.at[spot], sems.at[3 * g]),
        pltpu.make_async_copy(group.at[:, pl.ds(BLK, BLK)], rbuf.at[spot], sems.at[3 * g + 1]),
        pltpu.make_async_copy(group.at[:, pl.ds(2 * BLK, TAIL)], tails.at[spot], sems.at[3 * g + 2]),
    )


def load_terms(groups, lbuf, rbuf, tails, sems, vectors):
    copies = [
        group_copies(group, lbuf, rbuf, tails, sems, g) for g, group in enumerate(groups)
    ]
    for copy in copies[0][:2]:
        copy.start()
    for copy in [c[2] for c in copies] + vectors:
        copy.start()
    for pair in copies[1:]:
        for copy in pair[:2]:
            copy.start()


def read_blocks(groups, lbuf, rbuf, tails, sems, table_v, table, sem):
    for g, group in enumerate(groups):
        group_copies(group, lbuf, rbuf, tails, sems, g)[2].wait()
    table_v[...] = tails[:, 0, :128].astype(I32)
    move = pltpu.make_async_copy(table_v, table, sem)
    move.start()
    move.wait()


def build_and_apply(groups, lbuf, rbuf, tails, sems, table, lq_ref, rq_ref, vb, acc, done, ready):
    lq = lq_ref[...]
    lq_t = lq.T
    rq = rq_ref[...]
    rq_t = rq.T

    def some(g, carry):
        left, right, _ = group_copies(groups[0], lbuf, rbuf, tails, sems, g)
        left.wait()
        right.wait()
        spots = [4 * g + u for u in range(4)]
        temps = [(dot(lbuf[k], lq).astype(BF16), dot(rbuf[k], rq_t).astype(BF16)) for k in spots]
        lefts = [dot(lq_t, lt).astype(BF16) for lt, _ in temps]
        rights = [dot(rq, rt).astype(BF16) for _, rt in temps]
        for k, l, r in zip(spots, lefts, rights):
            lbuf[k] = l
            rbuf[k] = r
        done(g)
        pl.when(g == 0)(ready)
        terms = [(table[k, 0], table[k, 1]) for k in spots]
        apply_terms(terms, lefts, rights, vb, acc)
        return carry

    lax.fori_loop(0, len(groups), some, 0)


def part_kernel(count, carried, lq_ref, rq_ref, vb, *rest):
    if carried:
        h_in, rest = rest[0], rest[1:]
    groups, rest = rest[:count], rest[count:]
    lbuf, rbuf, table_out, hv = rest[:4]
    tails, table_v, table, sems = rest[4:]
    load_terms(groups, lbuf, rbuf, tails, sems, [])

    def clear(b, carry):
        hv[b] = h_in[b] if carried else jnp.zeros((BLK, BLK), F32)
        return carry

    lax.fori_loop(0, NB, clear, 0)
    table_copy = pltpu.make_async_copy(table_v, table_out, sems.at[3 * count + 1])

    def ready():
        read_blocks(groups, lbuf, rbuf, tails, sems, table_v, table, sems.at[3 * count])
        table_copy.start()

    build_and_apply(
        groups, lbuf, rbuf, tails, sems, table, lq_ref, rq_ref, vb, hv, lambda g: None, ready
    )
    table_copy.wait()


def part(groups, lq, rq, vb, h_in):
    count = len(groups)
    terms = 4 * count
    carried = h_in is not None

    def kernel(*refs):
        part_kernel(count, carried, *refs)

    env = jax.ShapeDtypeStruct((terms, BLK, BLK), BF16)
    return pl.pallas_call(
        kernel,
        out_shape=(
            env,
            env,
            jax.ShapeDtypeStruct((terms, 128), I32),
            jax.ShapeDtypeStruct(FULL, F32),
        ),
        in_specs=[VMEM] * (3 + carried) + [HBM] * count,
        out_specs=(VMEM, VMEM, HBM, VMEM),
        scratch_shapes=[
            pltpu.VMEM((terms, TAIL, BLK), BF16),
            pltpu.VMEM((terms, 128), I32),
            pltpu.SMEM((terms, 128), I32),
            pltpu.SemaphoreType.DMA((3 * count + 2,)),
        ],
        compiler_params=pltpu.CompilerParams(vmem_limit_bytes=24 * MIB),
        cost_estimate=LIGHT,
    )(lq, rq, vb, *((h_in,) if carried else ()), *groups)


def fold(p):
    return jnp.sum(p.reshape(BLK // 8, 8, BLK), axis=0)


def total(acc):
    return jnp.sum(jnp.sum(acc, axis=0, keepdims=True), axis=1, keepdims=True)


def solve_kernel(count, sizes, ids, lq_ref, rq_ref, scale_ref, psi_hbm, diag_hbm, vb_hbm, h_hbm, *rest):
    tables, rest = rest[: len(sizes)], rest[len(sizes):]
    envs, rest = rest[: 2 * len(sizes)], rest[2 * len(sizes):]
    groups, rest = rest[:count], rest[count:]
    out_ref = rest[0]
    lbuf, rbuf, tails, table_v, table, xv, hv, tv, gv, dv, vb, psi, sems, in_sems = rest[1:]
    op = ids[1]
    zero = jnp.zeros((8, BLK), F32)

    def over_blocks(step, sums):
        return lax.fori_loop(0, NB, step, (zero,) * sums)

    vectors = [
        pltpu.make_async_copy(source, target, in_sems.at[i])
        for i, (source, target) in enumerate(
            ((vb_hbm, vb), (h_hbm, hv), (psi_hbm.at[0], psi), (diag_hbm.at[0], dv))
        )
    ]
    load_terms(groups, lbuf, rbuf, tails, sems, vectors[:2])
    for copy in vectors[2:]:
        copy.start()
    built = []
    begin = 4 * count
    for i, size in enumerate(sizes):
        spot = pl.ds(begin, size)
        for j, (source, target) in enumerate(
            ((envs[2 * i], lbuf), (envs[2 * i + 1], rbuf), (tables[i], table))
        ):
            copy = pltpu.make_async_copy(source, target.at[spot], in_sems.at[4 + 3 * i + j])
            copy.start()
            built.append(copy)
        begin += size

    def ready():
        mine = table.at[pl.ds(0, 4 * count)]
        read_blocks(groups, lbuf, rbuf, tails, sems, table_v, mine, sems.at[3 * count])
        vectors[0].wait()
        vectors[1].wait()

    build_and_apply(
        groups, lbuf, rbuf, tails, sems, table, lq_ref, rq_ref, vb, hv, lambda g: None, ready
    )
    vectors[2].wait()
    vectors[3].wait()

    start_scale = scale_ref[0:1, 0:1]

    def finish_h(b, sums):
        x = psi[b].astype(F32) * start_scale
        h = hv[b] + dv[b] * x
        xv[b] = x
        hv[b] = h
        return (sums[0] + fold(x * h),)

    (theta_sum,) = over_blocks(finish_h, 1)
    theta = total(theta_sum)

    def residual(b, sums):
        x = xv[b]
        t = (hv[b] - theta * x) / dv[b]
        tv[b] = t
        return (sums[0] + fold(x * t),)

    (along,) = over_blocks(residual, 1)

    def orthogonal(along, b, sums):
        t = tv[b] - along * xv[b]
        tv[b] = t
        return (sums[0] + fold(t * t),)

    def rotation(theta, b, c):
        low = (c - theta) / 2 + jnp.sqrt(((theta - c) / 2) ** 2 + b * b)
        inv = 1.0 / jnp.sqrt(low * low + b * b)
        return low * inv, b * inv

    def over_terms(step, value, unroll=UNROLL):
        def some(i, value):
            spots = [i * unroll + u for u in range(unroll)]
            return step([(table[k, 0], table[k, 1]) for k in spots], spots, value)

        return lax.fori_loop(0, 64 // unroll, some, value)

    for step in range(ITERS - 1):
        (size,) = over_blocks(functools.partial(orthogonal, total(along)), 1)
        scale_t = lax.rsqrt(total(size) + 1e-12)

        def unit(b, sums):
            t = tv[b] * scale_t
            tv[b] = t
            vb[b] = t.astype(BF16)
            gv[b] = dv[b] * t
            return sums

        over_blocks(unit, 0)
        if step == 0:
            for copy in built:
                copy.wait()

        def apply_step(terms, spots, value):
            apply_terms(terms, [lbuf[k] for k in spots], [rbuf[k] for k in spots], vb, gv)
            return value

        over_terms(apply_step, 0, 2 * UNROLL)

        def couplings(b, sums):
            g = gv[b]
            t = tv[b]
            return (sums[0] + fold(xv[b] * g), sums[1] + fold(t * g), sums[2] + fold(t * hv[b]))

        sums = over_blocks(couplings, 3)
        cross, curve, back = (total(v) for v in sums)
        keep, move = rotation(theta, cross, curve)
        theta = keep * keep * theta - keep * move * (cross + back) + move * move * curve

        def turn(keep, move, theta, b, sums):
            x = keep * xv[b] - move * tv[b]
            h = keep * hv[b] - move * gv[b]
            xv[b] = x
            hv[b] = h
            t = (h - theta * x) / dv[b]
            tv[b] = t
            return (sums[0] + fold(x * t),)

        (along,) = over_blocks(functools.partial(turn, keep, move, theta), 1)

    along = total(along)

    def last_orthogonal(b, sums):
        t = tv[b] - along * xv[b]
        tv[b] = t
        t2 = t * t
        return (sums[0] + fold(t2), sums[1] + fold(hv[b] * t), sums[2] + fold(dv[b] * t2))

    size, cross, curve_diag = (total(v) for v in over_blocks(last_orthogonal, 3))
    scale_t = lax.rsqrt(size + 1e-12)

    def last_unit(b, sums):
        vb[b] = (tv[b] * scale_t).astype(BF16)
        return sums

    over_blocks(last_unit, 0)

    def last_step(terms, spots, acc):
        mids = [dot(vb[s], rbuf[k]).astype(BF16) for (s, _), k in zip(terms, spots)]
        for (_, d), k, f in zip(terms, spots, mids):
            acc = acc + fold(tv[d] * dot(lbuf[k], f))
        return acc

    curve_terms = over_terms(last_step, zero, 2 * UNROLL)
    curve = (curve_diag * scale_t + 2.0 * total(curve_terms)) * scale_t
    keep, move = rotation(theta, cross * scale_t, curve)
    move = move * scale_t
    amplitude = float(NB * BLK * BLK) ** 0.5
    out_ref[0, 0] = (keep * xv[op] - move * tv[op]) * amplitude


def solve(ids, parts, lq, rq, scale, psi, diagonal, vb, h, groups):
    count = len(groups)
    sizes = tuple(p[0].shape[0] for p in parts)

    def kernel(*refs):
        solve_kernel(count, sizes, *refs)

    return pl.pallas_call(
        kernel,
        out_shape=jax.ShapeDtypeStruct((1, 1, BLK, BLK), F32),
        in_specs=[SMEM] + [VMEM] * 3 + [HBM] * (4 + 3 * len(sizes) + count),
        out_specs=VMEM,
        scratch_shapes=[
            pltpu.VMEM((64, BLK, BLK), BF16),
            pltpu.VMEM((64, BLK, BLK), BF16),
            pltpu.VMEM((4 * count, TAIL, BLK), BF16),
            pltpu.VMEM((4 * count, 128), I32),
            pltpu.SMEM((64, 128), I32),
            pltpu.VMEM(FULL, F32),
            pltpu.VMEM(FULL, F32),
            pltpu.VMEM(FULL, F32),
            pltpu.VMEM(FULL, F32),
            pltpu.VMEM(FULL, F32),
            pltpu.VMEM(FULL, BF16),
            pltpu.VMEM(FULL, BF16),
            pltpu.SemaphoreType.DMA((3 * count + 1,)),
            pltpu.SemaphoreType.DMA((4 + 3 * len(sizes),)),
        ],
        compiler_params=pltpu.CompilerParams(vmem_limit_bytes=45 * MIB),
        cost_estimate=LIGHT,
    )(
        ids,
        lq,
        rq,
        scale,
        psi,
        diagonal,
        vb,
        h,
        *[p[2] for p in parts],
        *[env for p in parts for env in p[:2]],
        *groups,
    )


def start_kernel(psi_ref, vb_ref, scale_ref):
    def square(b, acc):
        v = psi_ref[0, b].astype(F32)
        return acc + fold(v * v)

    norm = lax.fori_loop(0, NB, square, jnp.zeros((8, BLK), F32))
    scale = lax.rsqrt(total(norm) + 1e-12)
    scale_ref[...] = jnp.broadcast_to(scale, (8, 128))

    def unit(b, carry):
        vb_ref[b] = (psi_ref[0, b].astype(F32) * scale).astype(BF16)
        return carry

    lax.fori_loop(0, NB, unit, 0)


def start_vector(psi):
    return pl.pallas_call(
        start_kernel,
        out_shape=(
            jax.ShapeDtypeStruct(FULL, BF16),
            jax.ShapeDtypeStruct((8, 128), F32),
        ),
        in_specs=[VMEM],
        out_specs=(VMEM, VMEM),
        compiler_params=pltpu.CompilerParams(vmem_limit_bytes=8 * MIB),
        cost_estimate=LIGHT,
    )(psi)


def after(values, marks):
    return lax.optimization_barrier((tuple(values), tuple(marks)))[0]


def body(psi, diagonal, left_step, right_step, left_env, right_env, src_block, dst_block):
    site = lax.axis_index("site")
    op = lax.axis_index("op")
    ids = jnp.stack([site, op]).astype(I32)
    core = site % 2

    blocks = jnp.stack([src_block, dst_block], 1).astype(BF16)
    tails = jnp.pad(blocks[:, None, :], ((0, 0), (0, TAIL - 1), (0, BLK - 2)))
    whole = jnp.concatenate([left_env, right_env, tails], 1)
    mine = lax.dynamic_slice_in_dim(whole, 2 * core, 2, 0)
    parts = (mine[:1], mine[1:])

    first = [swap_op(p, i, 0) for i, p in enumerate(parts)]
    steps = (left_step[0], right_step[0])
    other = tuple(swap_core(step) for step in steps)
    product = pair_product(ids, steps, other)

    two = [jnp.concatenate(pair, 0) for pair in zip(parts, first)]
    two, product = lax.optimization_barrier((two, product))
    second = [swap_op(p, i, 1) for i, p in enumerate(two)]
    received = []
    for k in (1, 2, 3):
        pairs = [(2 * y, 2 * (y + k)) for y in range(4 - k)]
        pairs += [(2 * y + 1, 2 * (y - k) + 1) for y in range(k, 4)]
        received.append(lax.ppermute(product, "site", pairs))

    four = [jnp.concatenate(pair, 0) for pair in zip(two, second)]
    third = [swap_op(p, i, 2) for i, p in enumerate(four)]
    psi, received = after((psi, tuple(received)), four)
    across = [swap_core(r) for r in received]
    vb, scale = start_vector(psi)
    lq, rq = chain_products(ids, other, received, across)
    old = [swap_op(p, i, 3) for i, p in enumerate(four)]

    def both(groups):
        return list(groups) + [swap_core(g) for g in groups]

    built = [part(both(four), lq, rq, vb, None)]
    third = after(third, built[-1][2:3])
    new = [swap_op(p, i, 3) for i, p in enumerate(third)]
    old = after(old, built[-1][2:3])
    built.append(part(both(third), lq, rq, vb, built[-1][3]))
    new = after(new, built[-1][2:3])
    return solve(ids, built, lq, rq, scale, psi, diagonal, vb, built[-1][3], both(old) + both(new))


def solution(mesh):
    placed = (
        P("site", None, None, None),
        P("site", None, None, None),
        P("site", None, None),
        P("site", None, None),
        P("op", None, None),
        P("op", None, None),
        P("op"),
        P("op"),
    )
    return jax.shard_map(
        body, mesh=mesh, in_specs=placed, out_specs=P("site", "op", None, None), check_vma=False
    )
```

```python
import functools

import jax
import jax.numpy as jnp
from jax import lax
from jax.experimental import pallas as pl
from jax.experimental.pallas import tpu as pltpu
from jax.sharding import PartitionSpec as P

ITERS = 2
BLK = 256
NB = 16
TAIL = 16
ROWS = 2 * BLK + TAIL
BF16 = jnp.bfloat16
F32 = jnp.float32
I32 = jnp.int32
HIGH = lax.Precision.HIGHEST
MIB = 1 << 20
FULL = (NB, BLK, BLK)

XA, XB, ZA, ZB = (1, 0), (3, 0), (0, 1), (0, 3)
ORDERS = (
    ((XA, ZA, XB, ZB), (ZA, XB, ZB, XA)),
    ((XB, ZB, XA, ZA), (ZB, XA, ZA, XB)),
)

LIGHT = pl.CostEstimate(flops=1, bytes_accessed=1, transcendentals=0)
SMEM = pl.BlockSpec(memory_space=pltpu.SMEM)
VMEM = pl.BlockSpec(memory_space=pltpu.VMEM)
HBM = pl.BlockSpec(memory_space=pl.ANY)


def swap_op(value, part, stage):
    pairs = []
    for site in range(8):
        mx, mz = ORDERS[site % 2][part][stage]
        for x in range(4):
            for z in range(4):
                pairs.append((site * 16 + x * 4 + z, site * 16 + (x ^ mx) * 4 + (z ^ mz)))
    return lax.ppermute(value, ("site", "op"), pairs)


def swap_core(value):
    return lax.ppermute(value, "site", [(i, i ^ 1) for i in range(8)])


def dot(a, b):
    return jnp.dot(a, b, preferred_element_type=F32)


def dot_nt(a, b):
    return lax.dot_general(a, b, (((1,), (1,)), ((), ())), preferred_element_type=F32)


def dot_tn(a, b):
    return lax.dot_general(a, b, (((0,), (0,)), ((), ())), preferred_element_type=F32)


def dot_high(a, b):
    return jnp.dot(a, b, precision=HIGH, preferred_element_type=F32)


def identity():
    rows = lax.broadcasted_iota(I32, (BLK, BLK), 0)
    cols = lax.broadcasted_iota(I32, (BLK, BLK), 1)
    return jnp.where(rows == cols, 1.0, 0.0).astype(F32)


def pair_kernel(site_ref, own_left, own_right, other_left, other_right, out_ref):
    eye = identity()
    first = site_ref[0] % 2 == 0
    a = jnp.where(first, own_left[...], other_right[...])
    b = jnp.where(first, other_left[...], own_right[...])
    out_ref[...] = dot_high(eye + 0.3 * a, eye + 0.3 * b)


def pair_product(site, own, other):
    return pl.pallas_call(
        pair_kernel,
        out_shape=jax.ShapeDtypeStruct((BLK, BLK), F32),
        in_specs=[SMEM] + [VMEM] * 4,
        out_specs=VMEM,
        cost_estimate=LIGHT,
    )(site, *own, *other)


def chain_kernel(site_ref, other_left, other_right, m1, m2, m3, n1, n2, n3, lq_ref, rq_ref):
    eye = identity()
    site = site_ref[0]
    core, y = site % 2, site // 2
    own, across = (m1, m2, m3), (n1, n2, n3)
    lefts, rights = [], []
    for k in range(3):
        left = jnp.where(core == 0, own[k][...], across[k][...])
        right = jnp.where(core == 0, across[k][...], own[k][...])
        lefts.append(jnp.where(y >= k + 1, left, eye))
        rights.append(jnp.where(y + k + 1 <= 3, right, eye))
    s_part = jnp.where(core == 1, eye + 0.3 * other_left[...], eye)
    t_part = jnp.where(core == 0, eye + 0.3 * other_right[...], eye)
    a = dot_high(lefts[2], lefts[1])
    b = dot_high(lefts[0], s_part)
    c = dot_high(t_part, rights[0])
    d = dot_high(rights[1], rights[2])
    lq_ref[...] = dot_high(a, b).astype(BF16)
    rq_ref[...] = dot_high(c, d).astype(BF16)


def chain_products(site, other, received, across):
    out = jax.ShapeDtypeStruct((BLK, BLK), BF16)
    return pl.pallas_call(
        chain_kernel,
        out_shape=(out, out),
        in_specs=[SMEM] + [VMEM] * 8,
        out_specs=(VMEM, VMEM),
        cost_estimate=LIGHT,
    )(site, *other, *received, *across)


UNROLL = 4


def apply_terms(terms, lefts, rights, vb, acc):
    mids = []
    for (s, d), r in zip(terms, rights):
        mids.append((dot(vb[s], r).astype(BF16), dot_nt(vb[d], r).astype(BF16)))
    for (s, d), l, (f, b) in zip(terms, lefts, mids):
        acc[d] += dot(l, f)
        acc[s] += dot_tn(l, b)


def group_copies(group, lbuf, rbuf, tails, sems, g):
    spot = pl.ds(4 * g, 4)
    return (
        pltpu.make_async_copy(group.at[:, pl.ds(0, BLK)], lbuf.at[spot], sems.at[3 * g]),
        pltpu.make_async_copy(group.at[:, pl.ds(BLK, BLK)], rbuf.at[spot], sems.at[3 * g + 1]),
        pltpu.make_async_copy(group.at[:, pl.ds(2 * BLK, TAIL)], tails.at[spot], sems.at[3 * g + 2]),
    )


def load_terms(groups, lbuf, rbuf, tails, sems, vectors):
    copies = [
        group_copies(group, lbuf, rbuf, tails, sems, g) for g, group in enumerate(groups)
    ]
    for copy in copies[0][:2]:
        copy.start()
    for copy in [c[2] for c in copies] + vectors:
        copy.start()
    for pair in copies[1:]:
        for copy in pair[:2]:
            copy.start()


def read_blocks(groups, lbuf, rbuf, tails, sems, table_v, table, sem):
    for g, group in enumerate(groups):
        group_copies(group, lbuf, rbuf, tails, sems, g)[2].wait()
    table_v[...] = tails[:, 0, :128].astype(I32)
    move = pltpu.make_async_copy(table_v, table, sem)
    move.start()
    move.wait()


def build_and_apply(groups, lbuf, rbuf, tails, sems, table, lq_ref, rq_ref, vb, acc, done, ready):
    lq = lq_ref[...]
    lq_t = lq.T
    rq = rq_ref[...]
    rq_t = rq.T

    def some(g, carry):
        left, right, _ = group_copies(groups[0], lbuf, rbuf, tails, sems, g)
        left.wait()
        right.wait()
        spots = [4 * g + u for u in range(4)]
        temps = [(dot(lbuf[k], lq).astype(BF16), dot(rbuf[k], rq_t).astype(BF16)) for k in spots]
        lefts = [dot(lq_t, lt).astype(BF16) for lt, _ in temps]
        rights = [dot(rq, rt).astype(BF16) for _, rt in temps]
        for k, l, r in zip(spots, lefts, rights):
            lbuf[k] = l
            rbuf[k] = r
        done(g)
        pl.when(g == 0)(ready)
        terms = [(table[k, 0], table[k, 1]) for k in spots]
        apply_terms(terms, lefts, rights, vb, acc)
        return carry

    lax.fori_loop(0, len(groups), some, 0)


def part_kernel(count, carried, lq_ref, rq_ref, vb, *rest):
    if carried:
        h_in, rest = rest[0], rest[1:]
    groups, rest = rest[:count], rest[count:]
    lbuf, rbuf, table_out, hv = rest[:4]
    tails, table_v, table, sems = rest[4:]
    load_terms(groups, lbuf, rbuf, tails, sems, [])

    def clear(b, carry):
        hv[b] = h_in[b] if carried else jnp.zeros((BLK, BLK), F32)
        return carry

    lax.fori_loop(0, NB, clear, 0)
    table_copy = pltpu.make_async_copy(table_v, table_out, sems.at[3 * count + 1])

    def ready():
        read_blocks(groups, lbuf, rbuf, tails, sems, table_v, table, sems.at[3 * count])
        table_copy.start()

    build_and_apply(
        groups, lbuf, rbuf, tails, sems, table, lq_ref, rq_ref, vb, hv, lambda g: None, ready
    )
    table_copy.wait()


def part(groups, lq, rq, vb, h_in):
    count = len(groups)
    terms = 4 * count
    carried = h_in is not None

    def kernel(*refs):
        part_kernel(count, carried, *refs)

    env = jax.ShapeDtypeStruct((terms, BLK, BLK), BF16)
    return pl.pallas_call(
        kernel,
        out_shape=(
            env,
            env,
            jax.ShapeDtypeStruct((terms, 128), I32),
            jax.ShapeDtypeStruct(FULL, F32),
        ),
        in_specs=[VMEM] * (3 + carried) + [HBM] * count,
        out_specs=(VMEM, VMEM, HBM, VMEM),
        scratch_shapes=[
            pltpu.VMEM((terms, TAIL, BLK), BF16),
            pltpu.VMEM((terms, 128), I32),
            pltpu.SMEM((terms, 128), I32),
            pltpu.SemaphoreType.DMA((3 * count + 2,)),
        ],
        compiler_params=pltpu.CompilerParams(vmem_limit_bytes=24 * MIB),
        cost_estimate=LIGHT,
    )(lq, rq, vb, *((h_in,) if carried else ()), *groups)


def fold(p):
    return jnp.sum(p.reshape(BLK // 8, 8, BLK), axis=0)


def total(acc):
    return jnp.sum(jnp.sum(acc, axis=0, keepdims=True), axis=1, keepdims=True)


def solve_kernel(count, sizes, ids, lq_ref, rq_ref, scale_ref, psi_hbm, diag_hbm, vb_hbm, h_hbm, *rest):
    tables, rest = rest[: len(sizes)], rest[len(sizes):]
    envs, rest = rest[: 2 * len(sizes)], rest[2 * len(sizes):]
    groups, rest = rest[:count], rest[count:]
    out_ref = rest[0]
    lbuf, rbuf, tails, table_v, table, xv, hv, tv, gv, dv, vb, psi, sems, in_sems = rest[1:]
    op = ids[1]
    zero = jnp.zeros((8, BLK), F32)

    def over_blocks(step, sums):
        return lax.fori_loop(0, NB, step, (zero,) * sums)

    vectors = [
        pltpu.make_async_copy(source, target, in_sems.at[i])
        for i, (source, target) in enumerate(
            ((vb_hbm, vb), (h_hbm, hv), (psi_hbm.at[0], psi), (diag_hbm.at[0], dv))
        )
    ]
    load_terms(groups, lbuf, rbuf, tails, sems, vectors[:2])
    for copy in vectors[2:]:
        copy.start()
    built = []
    begin = 4 * count
    for i, size in enumerate(sizes):
        spot = pl.ds(begin, size)
        for j, (source, target) in enumerate(
            ((envs[2 * i], lbuf), (envs[2 * i + 1], rbuf), (tables[i], table))
        ):
            copy = pltpu.make_async_copy(source, target.at[spot], in_sems.at[4 + 3 * i + j])
            copy.start()
            built.append(copy)
        begin += size

    def ready():
        mine = table.at[pl.ds(0, 4 * count)]
        read_blocks(groups, lbuf, rbuf, tails, sems, table_v, mine, sems.at[3 * count])
        vectors[0].wait()
        vectors[1].wait()

    build_and_apply(
        groups, lbuf, rbuf, tails, sems, table, lq_ref, rq_ref, vb, hv, lambda g: None, ready
    )
    vectors[2].wait()
    vectors[3].wait()

    start_scale = scale_ref[0:1, 0:1]

    def finish_h(b, sums):
        x = psi[b].astype(F32) * start_scale
        h = hv[b] + dv[b] * x
        xv[b] = x
        hv[b] = h
        return (sums[0] + fold(x * h),)

    (theta_sum,) = over_blocks(finish_h, 1)
    theta = total(theta_sum)

    def residual(b, sums):
        x = xv[b]
        t = (hv[b] - theta * x) / dv[b]
        tv[b] = t
        return (sums[0] + fold(x * t),)

    (along,) = over_blocks(residual, 1)

    def orthogonal(along, b, sums):
        t = tv[b] - along * xv[b]
        tv[b] = t
        return (sums[0] + fold(t * t),)

    def rotation(theta, b, c):
        low = (c - theta) / 2 + jnp.sqrt(((theta - c) / 2) ** 2 + b * b)
        inv = 1.0 / jnp.sqrt(low * low + b * b)
        return low * inv, b * inv

    def over_terms(step, value, unroll=UNROLL):
        def some(i, value):
            spots = [i * unroll + u for u in range(unroll)]
            return step([(table[k, 0], table[k, 1]) for k in spots], spots, value)

        return lax.fori_loop(0, 64 // unroll, some, value)

    for step in range(ITERS - 1):
        (size,) = over_blocks(functools.partial(orthogonal, total(along)), 1)
        scale_t = lax.rsqrt(total(size) + 1e-12)

        def unit(b, sums):
            t = tv[b] * scale_t
            tv[b] = t
            vb[b] = t.astype(BF16)
            gv[b] = dv[b] * t
            return sums

        over_blocks(unit, 0)
        if step == 0:
            for copy in built:
                copy.wait()

        def apply_step(terms, spots, value):
            apply_terms(terms, [lbuf[k] for k in spots], [rbuf[k] for k in spots], vb, gv)
            return value

        over_terms(apply_step, 0, 2 * UNROLL)

        def couplings(b, sums):
            g = gv[b]
            t = tv[b]
            return (sums[0] + fold(xv[b] * g), sums[1] + fold(t * g), sums[2] + fold(t * hv[b]))

        sums = over_blocks(couplings, 3)
        cross, curve, back = (total(v) for v in sums)
        keep, move = rotation(theta, cross, curve)
        theta = keep * keep * theta - keep * move * (cross + back) + move * move * curve

        def turn(keep, move, theta, b, sums):
            x = keep * xv[b] - move * tv[b]
            h = keep * hv[b] - move * gv[b]
            xv[b] = x
            hv[b] = h
            t = (h - theta * x) / dv[b]
            tv[b] = t
            return (sums[0] + fold(x * t),)

        (along,) = over_blocks(functools.partial(turn, keep, move, theta), 1)

    along = total(along)

    def last_orthogonal(b, sums):
        t = tv[b] - along * xv[b]
        tv[b] = t
        t2 = t * t
        return (sums[0] + fold(t2), sums[1] + fold(hv[b] * t), sums[2] + fold(dv[b] * t2))

    size, cross, curve_diag = (total(v) for v in over_blocks(last_orthogonal, 3))
    scale_t = lax.rsqrt(size + 1e-12)

    def last_unit(b, sums):
        vb[b] = (tv[b] * scale_t).astype(BF16)
        return sums

    over_blocks(last_unit, 0)

    def last_step(terms, spots, acc):
        mids = [dot(vb[s], rbuf[k]).astype(BF16) for (s, _), k in zip(terms, spots)]
        for (_, d), k, f in zip(terms, spots, mids):
            acc = acc + fold(tv[d] * dot(lbuf[k], f))
        return acc

    curve_terms = over_terms(last_step, zero, 4 * UNROLL)
    curve = (curve_diag * scale_t + 2.0 * total(curve_terms)) * scale_t
    keep, move = rotation(theta, cross * scale_t, curve)
    move = move * scale_t
    amplitude = float(NB * BLK * BLK) ** 0.5
    out_ref[0, 0] = (keep * xv[op] - move * tv[op]) * amplitude


def solve(ids, parts, lq, rq, scale, psi, diagonal, vb, h, groups):
    count = len(groups)
    sizes = tuple(p[0].shape[0] for p in parts)

    def kernel(*refs):
        solve_kernel(count, sizes, *refs)

    return pl.pallas_call(
        kernel,
        out_shape=jax.ShapeDtypeStruct((1, 1, BLK, BLK), F32),
        in_specs=[SMEM] + [VMEM] * 3 + [HBM] * (4 + 3 * len(sizes) + count),
        out_specs=VMEM,
        scratch_shapes=[
            pltpu.VMEM((64, BLK, BLK), BF16),
            pltpu.VMEM((64, BLK, BLK), BF16),
            pltpu.VMEM((4 * count, TAIL, BLK), BF16),
            pltpu.VMEM((4 * count, 128), I32),
            pltpu.SMEM((64, 128), I32),
            pltpu.VMEM(FULL, F32),
            pltpu.VMEM(FULL, F32),
            pltpu.VMEM(FULL, F32),
            pltpu.VMEM(FULL, F32),
            pltpu.VMEM(FULL, F32),
            pltpu.VMEM(FULL, BF16),
            pltpu.VMEM(FULL, BF16),
            pltpu.SemaphoreType.DMA((3 * count + 1,)),
            pltpu.SemaphoreType.DMA((4 + 3 * len(sizes),)),
        ],
        compiler_params=pltpu.CompilerParams(vmem_limit_bytes=45 * MIB),
        cost_estimate=LIGHT,
    )(
        ids,
        lq,
        rq,
        scale,
        psi,
        diagonal,
        vb,
        h,
        *[p[2] for p in parts],
        *[env for p in parts for env in p[:2]],
        *groups,
    )


def start_kernel(psi_ref, vb_ref, scale_ref):
    def square(b, acc):
        v = psi_ref[0, b].astype(F32)
        return acc + fold(v * v)

    norm = lax.fori_loop(0, NB, square, jnp.zeros((8, BLK), F32))
    scale = lax.rsqrt(total(norm) + 1e-12)
    scale_ref[...] = jnp.broadcast_to(scale, (8, 128))

    def unit(b, carry):
        vb_ref[b] = (psi_ref[0, b].astype(F32) * scale).astype(BF16)
        return carry

    lax.fori_loop(0, NB, unit, 0)


def start_vector(psi):
    return pl.pallas_call(
        start_kernel,
        out_shape=(
            jax.ShapeDtypeStruct(FULL, BF16),
            jax.ShapeDtypeStruct((8, 128), F32),
        ),
        in_specs=[VMEM],
        out_specs=(VMEM, VMEM),
        compiler_params=pltpu.CompilerParams(vmem_limit_bytes=8 * MIB),
        cost_estimate=LIGHT,
    )(psi)


def after(values, marks):
    return lax.optimization_barrier((tuple(values), tuple(marks)))[0]


def body(psi, diagonal, left_step, right_step, left_env, right_env, src_block, dst_block):
    site = lax.axis_index("site")
    op = lax.axis_index("op")
    ids = jnp.stack([site, op]).astype(I32)
    core = site % 2

    blocks = jnp.stack([src_block, dst_block], 1).astype(BF16)
    tails = jnp.pad(blocks[:, None, :], ((0, 0), (0, TAIL - 1), (0, BLK - 2)))
    whole = jnp.concatenate([left_env, right_env, tails], 1)
    mine = lax.dynamic_slice_in_dim(whole, 2 * core, 2, 0)
    parts = (mine[:1], mine[1:])

    first = [swap_op(p, i, 0) for i, p in enumerate(parts)]
    steps = (left_step[0], right_step[0])
    other = tuple(swap_core(step) for step in steps)
    product = pair_product(ids, steps, other)

    two = [jnp.concatenate(pair, 0) for pair in zip(parts, first)]
    two, product = lax.optimization_barrier((two, product))
    second = [swap_op(p, i, 1) for i, p in enumerate(two)]
    received = []
    for k in (1, 2, 3):
        pairs = [(2 * y, 2 * (y + k)) for y in range(4 - k)]
        pairs += [(2 * y + 1, 2 * (y - k) + 1) for y in range(k, 4)]
        received.append(lax.ppermute(product, "site", pairs))

    four = [jnp.concatenate(pair, 0) for pair in zip(two, second)]
    third = [swap_op(p, i, 2) for i, p in enumerate(four)]
    psi, received = after((psi, tuple(received)), four)
    across = [swap_core(r) for r in received]
    vb, scale = start_vector(psi)
    lq, rq = chain_products(ids, other, received, across)
    old = [swap_op(p, i, 3) for i, p in enumerate(four)]

    def both(groups):
        return list(groups) + [swap_core(g) for g in groups]

    built = [part(both(four), lq, rq, vb, None)]
    third = after(third, built[-1][2:3])
    new = [swap_op(p, i, 3) for i, p in enumerate(third)]
    old = after(old, built[-1][2:3])
    built.append(part(both(third), lq, rq, vb, built[-1][3]))
    new = after(new, built[-1][2:3])
    return solve(ids, built, lq, rq, scale, psi, diagonal, vb, built[-1][3], both(old) + both(new))


def solution(mesh):
    placed = (
        P("site", None, None, None),
        P("site", None, None, None),
        P("site", None, None),
        P("site", None, None),
        P("op", None, None),
        P("op", None, None),
        P("op"),
        P("op"),
    )
    return jax.shard_map(
        body, mesh=mesh, in_specs=placed, out_specs=P("site", "op", None, None), check_vma=False
    )
```
